256 devices in a mesh: dp: 64 (over x, z, core), mp: 4 (over y).
Axes of the slice: x: 4, y: 4, z: 8, core: 2. Of those that a mesh axis runs over, the one named last changes fastest.
Arguments:
- descriptors: bfloat16 [262144, 1024], P(('dp', 'mp')), may hold values from -440 to 440
- database: bfloat16 [524288, 1024], P(('dp', 'mp')), may hold values from -80 to 80
- anchor_row: int32 [256, 64, 24], P(('dp', 'mp')), may hold values from 0 to 1023
- partner_row: int32 [256, 64, 24], P(('dp', 'mp')), may hold values from 0 to 1023
- block_counts: int32 [256, 64], P(('dp', 'mp')), may hold values from 1 to 24, 1024 in all within a row
Outputs:
- whitened: bfloat16 [524288, 1024], P(('dp', 'mp'))
The draws below stay inside these ranges and needn't reach their ends.
Inputs may be any that keep to these rules, and one draw needn't show every extreme that they name: `block_counts`: the counts of one device add up to 1024; every device has a block with exactly 24 live pairs; slots from a block's count on are not pairs.
All inputs are finite; a program needn't handle non-finite values.
Results may differ from the reference program's by a relative error of at most 0.0015.
The reference program's roundings to bfloat16 on the way count: a program that leaves them out, or rounds other values in their place, can miss the bound.
Values may be sent and summed in bfloat16 or wider, within the bound.
A program may use at most 128 MiB of HBM per device.

```python
import math
import jax
import jax.numpy as jnp
import numpy as np
from jax import lax

D = 1024
R_DEV = 1024
PAIRS_DEV = 1024
DB_DEV = 2048
CAP = 24
ROWS = 262144
DB_ROWS = 524288
N_DP = 64
N_MP = 4
DEVICES = 256


def column_scales(key):
    return jnp.exp(jax.random.uniform(key, (1, D), minval=math.log(0.4), maxval=math.log(4.0)))


def draw_descriptors(key, part):
    col_scales = column_scales(key)
    key = jax.random.fold_in(key, 7)
    key_noise, key_rows, key_band = jax.random.split(key, 3)
    base_values = jnp.clip(jax.random.normal(key_noise, (ROWS, D)), -3.0, 3.0)
    row_scales = jnp.exp(jax.random.uniform(key_rows, (ROWS, 1), minval=math.log(0.4), maxval=math.log(4.0)))
    band_width = max(D // DEVICES, 1)
    band_total = D // band_width
    band_order = jax.random.permutation(key_band, DEVICES)
    row_owner = jnp.arange(ROWS, dtype=jnp.int32) // R_DEV
    target = band_order[row_owner][:, None]
    column_band = (jnp.arange(D, dtype=jnp.int32) // band_width)[None, :]
    boost_level = math.sqrt(DEVICES)
    boost_factor = jnp.where((column_band == target) & (target < band_total), boost_level, 1.0)
    return (0.5 * base_values * row_scales * col_scales * boost_factor).astype(jnp.bfloat16)


def draw_database(key, part):
    col_scales = column_scales(key)
    key = jax.random.fold_in(key, 9)
    key_noise, key_rows = jax.random.split(key, 2)
    base_values = jnp.clip(jax.random.normal(key_noise, (DB_ROWS, D)), -3.0, 3.0)
    row_scales = jnp.exp(jax.random.uniform(key_rows, (DB_ROWS, 1), minval=math.log(0.4), maxval=math.log(4.0)))
    return (1.5 * base_values * row_scales * col_scales).astype(jnp.bfloat16)


def touch_ends(array, rng, smallest, high):
    spot = [jax.random.randint(jax.random.fold_in(rng, axis), (), 0, length) for axis, length in enumerate(array.shape)]
    widest = array.shape.index(max(array.shape))
    neighbour = spot[:widest] + [(spot[widest] + 1) % array.shape[widest]] + spot[widest + 1:]
    return array.at[tuple(spot)].set(smallest).at[tuple(neighbour)].set(high)


def profile(amount, total, most, lean):
    portions = [(1 << 20) // math.isqrt(grade ** lean) + 1 for grade in range(2, amount + 1)]
    spare, holding = total - most - (amount - 1), [1] * (amount - 1)
    while spare > 0:
        free = [i for i in range(amount - 1) if holding[i] < most]
        mass, budget = sum([portions[i] for i in free]), spare
        for i in free:
            more = min(most - holding[i], max(1, budget * portions[i] // mass), spare)
            holding[i] = holding[i] + more
            spare = spare - more
    return np.array([most] + holding)


def uneven(rng, amount, total, bound, lean):
    if amount == 2:
        one = jax.random.randint(rng, (), max(1, total - bound), min(bound, total - 1) + 1)
        return jnp.stack([one, total - one])
    tallies = jnp.asarray(profile(amount, total, bound, lean), jnp.int32)
    couples = (amount - 1) // 2
    giver, taker = tallies[1:1 + 2 * couples:2], tallies[2:2 + 2 * couples:2]
    slack = jnp.minimum(giver - 1, bound - taker)
    shifted = jax.random.randint(jax.random.fold_in(rng, 1), (couples,), 0, 1 << 20) % (slack + 1)
    tallies = tallies.at[1:1 + 2 * couples:2].set(giver - shifted).at[2:2 + 2 * couples:2].set(taker + shifted)
    return tallies[jax.random.permutation(jax.random.fold_in(rng, 2), amount)]


def setup_inputs(seed: int = 0) -> dict:
    splits = jax.random.split(jax.random.key(seed), 6)
    return {
        "descriptors": draw_descriptors(jax.random.fold_in(splits[5], 71), 0),
        "database": draw_database(jax.random.fold_in(splits[5], 71), 0),
        "anchor_row": touch_ends(jax.random.randint(splits[2], (DEVICES, N_DP, CAP), 0, R_DEV), jax.random.fold_in(splits[2], 1), 0, R_DEV - 1).astype(jnp.int32),
        "partner_row": touch_ends(jax.random.randint(splits[3], (DEVICES, N_DP, CAP), 0, R_DEV), jax.random.fold_in(splits[3], 1), 0, R_DEV - 1).astype(jnp.int32),
        "block_counts": jax.vmap(lambda own: uneven(own, N_DP, PAIRS_DEV, CAP, 2))(jax.random.split(splits[4], DEVICES)).reshape((DEVICES, N_DP)).astype(jnp.int32),
    }


shrink_weight = 0.5
ridge_term = 0.05
norm_epsilon = 1e-06
contract_rows = (((0,), (0,)), ((), ()))

def reference(descriptors, database, anchor_row, partner_row, block_counts):
    devices = N_DP * N_MP
    slot_iota = jnp.arange(CAP, dtype=jnp.int32)[None, :]
    owner_base = jnp.arange(N_DP, dtype=jnp.int32) * N_MP

    def pair_terms(running, device):
        first_row = (device * R_DEV).astype(jnp.int32)
        own_rows = lax.dynamic_slice_in_dim(descriptors, first_row, R_DEV, 0)
        anchors = jnp.take(own_rows, anchor_row[device].reshape(-1), axis=0)
        owners = owner_base + device % N_MP
        partner_at = (owners[:, None] * R_DEV + partner_row[device]).reshape(-1)
        partners = jnp.take(descriptors, partner_at, axis=0)
        live_slots = (slot_iota < block_counts[device][:, None]).reshape(-1)
        differences = jnp.where(live_slots[:, None], anchors.astype(jnp.float32) - partners.astype(jnp.float32), 0.0)
        pair_flat = differences.astype(jnp.bfloat16)
        return (running + lax.dot_general(pair_flat.astype(jnp.float32), pair_flat.astype(jnp.float32), contract_rows, preferred_element_type=jnp.float32), None)
    pair_sum, _ = lax.scan(pair_terms, jnp.zeros((D, D), jnp.float32), jnp.arange(devices, dtype=jnp.int32))
    row_sum = lax.dot_general(descriptors.astype(jnp.float32), descriptors.astype(jnp.float32), contract_rows, preferred_element_type=jnp.float32)
    col_total = lax.optimization_barrier(jnp.sum(descriptors, axis=0, dtype=jnp.float32))
    pairs_all = PAIRS_DEV * devices
    rows_all = R_DEV * devices
    col_mean = col_total / rows_all
    metric = pair_sum / pairs_all + shrink_weight / rows_all * row_sum
    metric = metric - shrink_weight * col_mean[:, None] * col_mean[None, :] + ridge_term * jnp.eye(D, dtype=jnp.float32)
    factor = jnp.linalg.cholesky(metric)
    inverse_t = lax.linalg.triangular_solve(factor, jnp.eye(D, dtype=jnp.float32), left_side=True, lower=True, transpose_a=True).astype(jnp.bfloat16)

    def whiten(db_block):
        centered = (db_block.astype(jnp.float32) - col_mean).astype(jnp.bfloat16)
        projected = jnp.dot(centered.astype(jnp.float32), inverse_t.astype(jnp.float32), preferred_element_type=jnp.float32)
        row_scale = lax.rsqrt(lax.optimization_barrier(jnp.mean(projected * projected, axis=1, keepdims=True)) + norm_epsilon)
        return (projected * row_scale).astype(jnp.bfloat16)
    db_blocks = database.reshape(devices, DB_DEV, D)
    return lax.map(whiten, db_blocks).reshape(devices * DB_DEV, D)
```

```python
import jax
import jax.numpy as jnp
from jax import lax
from jax.experimental import pallas as pl
from jax.experimental.pallas import tpu as pltpu
from jax.sharding import PartitionSpec as P

PAIRS_DEV = 1024


shrink_weight = 0.5
ridge_term = 0.05
norm_epsilon = 1e-06
contract_rows = (((0,), (0,)), ((), ()))

N = 1024
NB = 128
F32 = jnp.float32
HI = lax.Precision.HIGHEST

def lane_bcast(x, c):
    return jnp.broadcast_to(x[:, c:c + 1], x.shape)

def row_bcast(x, i):
    return jnp.broadcast_to(x[i:i + 1, :], x.shape)

def factor_block(rows):
    lane = lax.broadcasted_iota(jnp.int32, (8, NB), 1)
    count = len(rows)
    for q in range(count):
        base = 8 * q
        inside = (lane >= base) & (lane < base + 8)
        cur = rows[q]
        cols = [lane_bcast(cur, base + j) for j in range(8)]
        d = {}
        for j in range(8):
            for i in range(j, 8):
                d[i, j] = row_bcast(cols[j], i)
        w = [jnp.where(inside, jnp.where(lane == base + i, 1.0, 0.0), row_bcast(cur, i)) for i in range(8)]
        inv, l, rs = [], {}, []
        for j in range(8):
            p = d[j, j]
            r = 1.0 / p
            inv.append(r)
            rs.append(lax.rsqrt(p))
            for i in range(j + 1, 8):
                l[i, j] = d[i, j] * r
            for i in range(j + 1, 8):
                for k in range(j + 1, i + 1):
                    d[i, k] = d[i, k] - l[i, j] * d[k, j]
            for i in range(j + 1, 8):
                w[i] = w[i] - l[i, j] * w[j]
        g = [None] * 8
        for i in range(7, -1, -1):
            acc = inv[i] * w[i]
            for j in range(i + 1, 8):
                acc = acc - l[j, i] * g[j]
            g[i] = acc
        sub = lax.broadcasted_iota(jnp.int32, (8, NB), 0)
        out = rs[0] * w[0]
        for i in range(1, 8):
            out = jnp.where(sub == i, rs[i] * w[i], out)
        rows[q] = out
        for t in range(q + 1, count):
            acc = jnp.where(inside, 0.0, rows[t])
            for j in range(8):
                acc = acc - lane_bcast(rows[t], base + j) * g[j]
            rows[t] = acc
    return rows

def chol_kernel(m_ref, out_ref, c_ref, t_ref):
    c_ref[...] = m_ref[...]
    blocks = N // NB
    row = lax.broadcasted_iota(jnp.int32, (NB, NB), 0)
    col = lax.broadcasted_iota(jnp.int32, (NB, NB), 1)

    def step(k, _):
        off = pl.multiple_of(k * NB, NB)
        diag = c_ref.at[pl.ds(off, NB), pl.ds(off, NB)]
        rows = [diag[8 * q:8 * q + 8, :] for q in range(16)]
        rows = factor_block(rows)
        for q in range(16):
            t_ref[8 * q:8 * q + 8, :] = rows[q]
        t = jnp.where(row >= col, t_ref[...], 0.0)
        ck = jnp.dot(t, c_ref[pl.ds(off, NB), :], precision=HI, preferred_element_type=F32)
        c_ref[pl.ds(off, NB), :] = ck
        c_ref[pl.ds(off, NB), pl.ds(off, NB)] = t

        def update(i, _):
            io = pl.multiple_of(i * NB, NB)
            u = c_ref[pl.ds(off, NB), pl.ds(io, NB)]
            c_ref[pl.ds(io, NB), pl.ds(off, NB)] = jnp.zeros((NB, NB), F32)
            prod = lax.dot_general(u, c_ref[pl.ds(off, NB), :], (((0,), (0,)), ((), ())),
                                   precision=HI, preferred_element_type=F32)
            c_ref[pl.ds(io, NB), :] = c_ref[pl.ds(io, NB), :] - prod
            return 0
        lax.fori_loop(k + 1, blocks, update, 0)
        return 0
    lax.fori_loop(0, blocks, step, 0)
    for i in range(blocks):
        r = lax.broadcasted_iota(jnp.int32, (NB, N), 0) + i * NB
        c = lax.broadcasted_iota(jnp.int32, (NB, N), 1)
        out_ref[i * NB:(i + 1) * NB, :] = jnp.where(r >= c, c_ref[i * NB:(i + 1) * NB, :], 0.0).astype(out_ref.dtype)


def inverse_factor(metric):
    return pl.pallas_call(
        chol_kernel,
        out_shape=jax.ShapeDtypeStruct((N, N), jnp.bfloat16),
        in_specs=[pl.BlockSpec(memory_space=pltpu.VMEM)],
        out_specs=pl.BlockSpec(memory_space=pltpu.VMEM),
        scratch_shapes=[pltpu.VMEM((N, N), F32), pltpu.VMEM((NB, NB), F32)],
        compiler_params=pltpu.CompilerParams(vmem_limit_bytes=40 << 20),
    )(metric)


def whiten_kernel(db_ref, mean_ref, inv_ref, out_ref):
    centered = (db_ref[...].astype(F32) - mean_ref[0:1, :]).astype(jnp.bfloat16)
    projected = lax.dot_general(
        centered, inv_ref[...], (((1,), (1,)), ((), ())), preferred_element_type=F32
    )
    energy = jnp.mean(projected * projected, axis=1, keepdims=True)
    out_ref[...] = (projected * lax.rsqrt(energy + norm_epsilon)).astype(jnp.bfloat16)


def whiten(database, col_mean, inverse):
    rows, width = database.shape
    tile = 256
    return pl.pallas_call(
        whiten_kernel,
        grid=(rows // tile,),
        out_shape=jax.ShapeDtypeStruct((rows, width), jnp.bfloat16),
        in_specs=[
            pl.BlockSpec((tile, width), lambda i: (i, 0)),
            pl.BlockSpec((8, width), lambda i: (0, 0)),
            pl.BlockSpec((width, width), lambda i: (0, 0)),
        ],
        out_specs=pl.BlockSpec((tile, width), lambda i: (i, 0)),
        compiler_params=pltpu.CompilerParams(vmem_limit_bytes=40 << 20),
    )(database, jnp.broadcast_to(col_mean[None, :], (8, width)), inverse)


def shards(descriptors, database, anchor_row, partner_row, block_counts):
    feature_width = descriptors.shape[1]
    local_rows = descriptors.shape[0]
    peer_count = partner_row.shape[1]
    slot_count = partner_row.shape[2]
    devices = lax.axis_size("dp") * lax.axis_size("mp")
    pairs_all = PAIRS_DEV * devices
    rows_all = local_rows * devices
    slot_iota = lax.broadcasted_iota(jnp.int32, (peer_count, slot_count), 1)
    live_slots = slot_iota < block_counts[0][:, None]
    wanted = jnp.where(live_slots, partner_row[0], -1)
    anchors = descriptors.at[anchor_row[0].reshape(-1)].get(mode="promise_in_bounds").reshape(
        peer_count, slot_count, feature_width
    )
    wanted_here = lax.all_to_all(wanted, "dp", split_axis=0, concat_axis=0, tiled=True)
    anchors_here = lax.all_to_all(anchors, "dp", split_axis=0, concat_axis=0, tiled=True)
    partners = descriptors.at[jnp.maximum(wanted_here, 0).reshape(-1)].get(
        mode="promise_in_bounds"
    ).reshape(peer_count, slot_count, feature_width)
    differences = jnp.where(
        wanted_here[:, :, None] >= 0, anchors_here.astype(F32) - partners.astype(F32), 0.0
    )
    pair_flat = differences.astype(jnp.bfloat16).reshape(-1, feature_width)
    col_sum = jnp.sum(descriptors, axis=0, dtype=F32)
    pair_gram = lax.dot_general(pair_flat, pair_flat, contract_rows, preferred_element_type=F32)
    row_gram = lax.dot_general(
        descriptors, descriptors, contract_rows, preferred_element_type=F32
    )
    partial_sum = pair_gram * (1.0 / pairs_all) + row_gram * (shrink_weight / rows_all)
    summed, col_total = lax.psum((partial_sum, col_sum), ("dp", "mp"))
    col_mean = col_total / rows_all
    identity = jnp.eye(feature_width, dtype=F32)
    metric = summed - shrink_weight * col_mean[:, None] * col_mean[None, :] + ridge_term * identity
    return whiten(database, col_mean, inverse_factor(metric))


def solution(mesh):
    placed = (
        P(("dp", "mp"), None),
        P(("dp", "mp"), None),
        P(("dp", "mp"), None, None),
        P(("dp", "mp"), None, None),
        P(("dp", "mp"), None),
    )
    return jax.shard_map(
        shards, mesh=mesh, in_specs=placed, out_specs=P(("dp", "mp"), None), check_vma=False
    )
```

```python
import jax
import jax.numpy as jnp
from jax import lax
from jax.experimental import pallas as pl
from jax.experimental.pallas import tpu as pltpu
from jax.sharding import PartitionSpec as P

PAIRS_DEV = 1024
R_ALL = 262144


shrink_weight = 0.5
ridge_term = 0.05
norm_epsilon = 1e-06
contract_rows = (((0,), (0,)), ((), ()))

N = 1024
NB = 128
F32 = jnp.float32
HI = lax.Precision.HIGHEST

def lane_bcast(x, c):
    return jnp.broadcast_to(x[:, c:c + 1], x.shape)

def row_bcast(x, i):
    return jnp.broadcast_to(x[i:i + 1, :], x.shape)

def factor_block(rows):
    lane = lax.broadcasted_iota(jnp.int32, (8, NB), 1)
    count = len(rows)
    for q in range(count):
        base = 8 * q
        inside = (lane >= base) & (lane < base + 8)
        cur = rows[q]
        cols = [lane_bcast(cur, base + j) for j in range(8)]
        d = {}
        for j in range(8):
            for i in range(j, 8):
                d[i, j] = row_bcast(cols[j], i)
        w = [jnp.where(inside, jnp.where(lane == base + i, 1.0, 0.0), row_bcast(cur, i)) for i in range(8)]
        inv, l, rs = [], {}, []
        for j in range(8):
            p = d[j, j]
            r = 1.0 / p
            inv.append(r)
            rs.append(lax.rsqrt(p))
            for i in range(j + 1, 8):
                l[i, j] = d[i, j] * r
            for i in range(j + 1, 8):
                for k in range(j + 1, i + 1):
                    d[i, k] = d[i, k] - l[i, j] * d[k, j]
            for i in range(j + 1, 8):
                w[i] = w[i] - l[i, j] * w[j]
        g = [None] * 8
        for i in range(7, -1, -1):
            acc = inv[i] * w[i]
            for j in range(i + 1, 8):
                acc = acc - l[j, i] * g[j]
            g[i] = acc
        sub = lax.broadcasted_iota(jnp.int32, (8, NB), 0)
        out = rs[0] * w[0]
        for i in range(1, 8):
            out = jnp.where(sub == i, rs[i] * w[i], out)
        rows[q] = out
        for t in range(q + 1, count):
            acc = jnp.where(inside, 0.0, rows[t])
            for j in range(8):
                acc = acc - lane_bcast(rows[t], base + j) * g[j]
            rows[t] = acc
    return rows


NX, NY, NZ, NC = 4, 4, 8, 2
PLANE = NX * NY
BLOCKS = N // NB
UPPER = [(i, j) for i in range(BLOCKS) for j in range(i, BLOCKS)]
DATA = len(UPPER) * NB // (NC * PLANE)
UNIT = DATA + 8
HALF = PLANE * UNIT
PIECE = 24
SEG = 16


def segments():
    found = []
    for b, (i, j) in enumerate(UPPER):
        for s in range(0, NB, SEG):
            flat = b * NB + s
            unit, inside = flat // DATA, flat % DATA
            found.append((i, j, s, unit * UNIT + inside))
    return found


def gram_kernel(pair_scale, row_scale, here_ref, part_ref, live_ref, desc_ref, out_ref, diff_ref, gram_ref):
    slots = here_ref.shape[0]
    tile = 256
    for r in range(0, slots, tile):
        gap = here_ref[r:r + tile, :].astype(F32) - part_ref[r:r + tile, :].astype(F32)
        keep = jnp.broadcast_to(live_ref[r:r + tile, 0:1], gap.shape)
        diff_ref[r:r + tile, :] = jnp.where(keep > 0.5, gap, 0.0).astype(jnp.bfloat16)
    for i in range(0, N, tile):
        pair = lax.dot_general(diff_ref[:, i:i + tile], diff_ref[:, i:], contract_rows, preferred_element_type=F32)
        row = lax.dot_general(desc_ref[:, i:i + tile], desc_ref[:, i:], contract_rows, preferred_element_type=F32)
        gram_ref[i:i + tile, i:] = pair * pair_scale + row * row_scale
    for i, j, s, at in segments():
        out_ref[at:at + SEG, :] = gram_ref[i * NB + s:i * NB + s + SEG, j * NB:(j + 1) * NB]
    ones = jnp.ones((8, desc_ref.shape[0]), jnp.bfloat16)
    sums = jnp.dot(ones, desc_ref[...], preferred_element_type=F32)
    sub = lax.broadcasted_iota(jnp.int32, (8, NB), 0)
    packed = sums[:, 0:NB]
    for i in range(1, BLOCKS):
        packed = jnp.where(sub == i, sums[:, i * NB:(i + 1) * NB], packed)
    for u in range(NC * PLANE):
        out_ref[u * UNIT + DATA:(u + 1) * UNIT, :] = packed


def gram(pair_scale, row_scale, here, partners, live, descriptors):
    return pl.pallas_call(
        lambda *refs: gram_kernel(pair_scale, row_scale, *refs),
        out_shape=jax.ShapeDtypeStruct((NC * HALF, NB), F32),
        in_specs=[pl.BlockSpec(memory_space=pltpu.VMEM)] * 4,
        out_specs=pl.BlockSpec(memory_space=pltpu.VMEM),
        scratch_shapes=[pltpu.VMEM(here.shape, jnp.bfloat16), pltpu.VMEM((N, N), F32)],
        compiler_params=pltpu.CompilerParams(vmem_limit_bytes=48 << 20),
    )(here, partners, live, descriptors)


def reduce_kernel(p_ref, out_ref, half, r0, r1, zb, r2, gz, s0, q0, s1, q1, s2, q2, s3, q3, s4, q4, s5, q5):
    dp, y = lax.axis_index("dp"), lax.axis_index("mp")
    core, z, x = dp % NC, (dp // NC) % NZ, dp // (NC * NZ)
    sibling = (dp + 1 - 2 * core, y)
    mine = x * NY + y

    def plane(o):
        return (x + o // NY) % NX, (y + o % NY) % NY

    def plane_from(o):
        return (x + NX - o // NY) % NX, (y + NY - o % NY) % NY

    def plane_id(o):
        tx, ty = plane(o)
        return ((tx * NZ + z) * NC + core, ty)

    def line_id(o):
        return ((x * NZ + (z + o) % NZ) * NC + core, y)

    def rows(base, count):
        return pl.ds(pl.multiple_of(base, 8), count)

    def send(src, dst, ssem, rsem, target):
        return pltpu.make_async_remote_copy(
            src_ref=src, dst_ref=dst, send_sem=ssem, recv_sem=rsem,
            device_id=target, device_id_type=pl.DeviceIdType.MESH,
        )

    barrier = pltpu.get_barrier_semaphore()
    pl.semaphore_signal(barrier, inc=1, device_id=sibling, device_id_type=pl.DeviceIdType.MESH)

    @pl.loop(1, PLANE)
    def _(o):
        pl.semaphore_signal(barrier, inc=1, device_id=plane_id(o), device_id_type=pl.DeviceIdType.MESH)

    @pl.loop(1, NZ)
    def _(o):
        pl.semaphore_signal(barrier, inc=1, device_id=line_id(o), device_id_type=pl.DeviceIdType.MESH)

    pl.semaphore_wait(barrier, 1 + (PLANE - 1) + (NZ - 1))

    def unit_at(o):
        tx, ty = plane(o)
        return (tx * NY + ty) * UNIT

    def copy0(o):
        at = unit_at(o)
        return send(p_ref.at[rows((1 - core) * HALF + at, UNIT)], r0.at[rows(at, UNIT)], s0.at[o], q0.at[o], sibling)

    def copy1(o):
        return send(half.at[rows(unit_at(o), UNIT)], r1.at[o], s1.at[o], q1.at[o], plane_id(o))

    @pl.loop(0, PLANE)
    def _(i):
        copy0((i + 1) % PLANE).start()

    zb[UNIT:, :] = jnp.zeros((zb.shape[0] - UNIT, NB), F32)

    @pl.loop(1, PLANE)
    def _(o):
        copy0(o).wait_recv()
        at = unit_at(o)
        half[rows(at, UNIT), :] = p_ref[rows(core * HALF + at, UNIT), :] + r0[rows(at, UNIT), :]
        copy1(o).start()

    copy0(0).wait_recv()
    at = mine * UNIT
    zb[0:UNIT, :] = p_ref[rows(core * HALF + at, UNIT), :] + r0[rows(at, UNIT), :]

    @pl.loop(1, PLANE)
    def _(o):
        copy1(o).wait_recv()
        zb[0:UNIT, :] = zb[0:UNIT, :] + r1[o]

    def copy2(o):
        return send(zb.at[rows(((z + o) % NZ) * PIECE, PIECE)], r2.at[o], s2.at[o], q2.at[o], line_id(o))

    def copy3(o, owner):
        piece = gz.at[rows(owner * PIECE, PIECE)]
        return send(piece, piece, s3.at[o], q3.at[o], line_id(o))

    @pl.loop(1, NZ)
    def _(o):
        copy2(o).start()

    own = rows(z * PIECE, PIECE)
    gz[own, :] = zb[own, :]

    @pl.loop(1, NZ)
    def _(o):
        copy2(o).wait_recv()
        gz[own, :] = gz[own, :] + r2[o]

    @pl.loop(1, NZ)
    def _(o):
        copy3(o, z).start()

    @pl.loop(1, NZ)
    def _(o):
        copy3(o, (z + NZ - o) % NZ).wait_recv()

    def copy4(o, unit):
        return send(gz.at[pl.ds(0, UNIT)], out_ref.at[rows(core * HALF + unit * UNIT, UNIT)], s4.at[o], q4.at[o], plane_id(o))

    def copy5(o, which):
        tx, ty = plane_from(o)
        piece = out_ref.at[rows(which * HALF + (tx * NY + ty) * UNIT, UNIT)]
        return send(piece, piece, s5.at[o], q5.at[o], sibling)

    @pl.loop(1, PLANE)
    def _(o):
        copy4(o, mine).start()

    out_ref[rows(core * HALF + mine * UNIT, UNIT), :] = gz[0:UNIT, :]
    copy5(0, core).start()

    @pl.loop(1, PLANE)
    def _(o):
        tx, ty = plane_from(o)
        copy4(o, tx * NY + ty).wait_recv()
        copy5(o, core).start()

    @pl.loop(0, PLANE)
    def _(o):
        copy5(o, 1 - core).wait_recv()
        copy5(o, core).wait_send()
        copy0(o).wait_send()

    @pl.loop(1, PLANE)
    def _(o):
        copy1(o).wait_send()
        copy4(o, mine).wait_send()

    @pl.loop(1, NZ)
    def _(o):
        copy2(o).wait_send()
        copy3(o, z).wait_send()


def reduce_all(packed):
    dma = pltpu.SemaphoreType.DMA
    return pl.pallas_call(
        reduce_kernel,
        out_shape=jax.ShapeDtypeStruct((NC * HALF, NB), F32),
        in_specs=[pl.BlockSpec(memory_space=pltpu.VMEM)],
        out_specs=pl.BlockSpec(memory_space=pltpu.VMEM),
        scratch_shapes=[
            pltpu.VMEM((HALF, NB), F32),
            pltpu.VMEM((HALF, NB), F32),
            pltpu.VMEM((PLANE, UNIT, NB), F32),
            pltpu.VMEM((NZ * PIECE, NB), F32),
            pltpu.VMEM((NZ, PIECE, NB), F32),
            pltpu.VMEM((NZ * PIECE, NB), F32),
        ] + [dma((PLANE,))] * 4 + [dma((NZ,))] * 4 + [dma((PLANE,))] * 4,
        compiler_params=pltpu.CompilerParams(
            collective_id=1, has_side_effects=True, vmem_limit_bytes=40 << 20
        ),
    )(packed)


def chol_kernel(p_ref, out_ref, mean_ref, c_ref, t_ref):
    rows_all = R_ALL
    c_ref[...] = jnp.zeros((N, N), F32)
    mean_ref[...] = jnp.zeros((8, N), F32)
    means = p_ref[DATA:UNIT, :] * (1.0 / rows_all)
    for i in range(BLOCKS):
        mean_ref[0:1, i * NB:(i + 1) * NB] = means[i:i + 1, :]
    for i, j, s, at in segments():
        c_ref[i * NB + s:i * NB + s + SEG, j * NB:(j + 1) * NB] = p_ref[at:at + SEG, :]
    row = lax.broadcasted_iota(jnp.int32, (NB, NB), 0)
    col = lax.broadcasted_iota(jnp.int32, (NB, NB), 1)
    for i in range(BLOCKS):
        a = i * NB
        outer = lax.dot_general(mean_ref[:, a:a + NB], mean_ref[:, a:], contract_rows,
                                precision=HI, preferred_element_type=F32)
        c_ref[a:a + NB, a:] = c_ref[a:a + NB, a:] - shrink_weight * outer
        c_ref[a:a + NB, a:a + NB] = c_ref[a:a + NB, a:a + NB] + jnp.where(row == col, ridge_term, 0.0)
    blocks = BLOCKS

    def step(k, _):
        off = pl.multiple_of(k * NB, NB)
        diag = c_ref.at[pl.ds(off, NB), pl.ds(off, NB)]
        rows = [diag[8 * q:8 * q + 8, :] for q in range(16)]
        rows = factor_block(rows)
        for q in range(16):
            t_ref[8 * q:8 * q + 8, :] = rows[q]
        t = jnp.where(row >= col, t_ref[...], 0.0)
        ck = jnp.dot(t, c_ref[pl.ds(off, NB), :], precision=HI, preferred_element_type=F32)
        c_ref[pl.ds(off, NB), :] = ck
        c_ref[pl.ds(off, NB), pl.ds(off, NB)] = t

        def update(i, _):
            io = pl.multiple_of(i * NB, NB)
            u = c_ref[pl.ds(off, NB), pl.ds(io, NB)]
            c_ref[pl.ds(io, NB), pl.ds(off, NB)] = jnp.zeros((NB, NB), F32)
            prod = lax.dot_general(u, c_ref[pl.ds(off, NB), :], (((0,), (0,)), ((), ())),
                                   precision=HI, preferred_element_type=F32)
            c_ref[pl.ds(io, NB), :] = c_ref[pl.ds(io, NB), :] - prod
            return 0
        lax.fori_loop(k + 1, blocks, update, 0)
        return 0
    lax.fori_loop(0, blocks, step, 0)
    for i in range(blocks):
        r = lax.broadcasted_iota(jnp.int32, (NB, N), 0) + i * NB
        c = lax.broadcasted_iota(jnp.int32, (NB, N), 1)
        out_ref[i * NB:(i + 1) * NB, :] = jnp.where(r >= c, c_ref[i * NB:(i + 1) * NB, :], 0.0).astype(out_ref.dtype)


def inverse_factor(packed):
    return pl.pallas_call(
        chol_kernel,
        out_shape=[jax.ShapeDtypeStruct((N, N), jnp.bfloat16), jax.ShapeDtypeStruct((8, N), F32)],
        in_specs=[pl.BlockSpec(memory_space=pltpu.VMEM)],
        out_specs=[pl.BlockSpec(memory_space=pltpu.VMEM)] * 2,
        scratch_shapes=[pltpu.VMEM((N, N), F32), pltpu.VMEM((NB, NB), F32)],
        compiler_params=pltpu.CompilerParams(vmem_limit_bytes=40 << 20),
    )(packed)


def whiten_kernel(db_ref, mean_ref, inv_ref, out_ref):
    centered = (db_ref[...].astype(F32) - mean_ref[0:1, :]).astype(jnp.bfloat16)
    projected = lax.dot_general(
        centered, inv_ref[...], (((1,), (1,)), ((), ())), preferred_element_type=F32
    )
    energy = jnp.mean(projected * projected, axis=1, keepdims=True)
    out_ref[...] = (projected * lax.rsqrt(energy + norm_epsilon)).astype(jnp.bfloat16)


def whiten(database, col_mean, inverse):
    rows, width = database.shape
    tile = 256
    return pl.pallas_call(
        whiten_kernel,
        grid=(rows // tile,),
        out_shape=jax.ShapeDtypeStruct((rows, width), jnp.bfloat16),
        in_specs=[
            pl.BlockSpec((tile, width), lambda i: (i, 0)),
            pl.BlockSpec((8, width), lambda i: (0, 0)),
            pl.BlockSpec((width, width), lambda i: (0, 0)),
        ],
        out_specs=pl.BlockSpec((tile, width), lambda i: (i, 0)),
        compiler_params=pltpu.CompilerParams(vmem_limit_bytes=40 << 20),
    )(database, col_mean, inverse)


def shards(descriptors, database, anchor_row, partner_row, block_counts):
    feature_width = descriptors.shape[1]
    local_rows = descriptors.shape[0]
    peer_count = partner_row.shape[1]
    slot_count = partner_row.shape[2]
    devices = lax.axis_size("dp") * lax.axis_size("mp")
    pairs_all = PAIRS_DEV * devices
    rows_all = local_rows * devices
    slot_iota = lax.broadcasted_iota(jnp.int32, (peer_count, slot_count), 1)
    live_slots = slot_iota < block_counts[0][:, None]
    wanted = jnp.where(live_slots, partner_row[0], -1)
    anchors = descriptors.at[anchor_row[0].reshape(-1)].get(mode="promise_in_bounds").reshape(
        peer_count, slot_count, feature_width
    )
    wanted_here = lax.all_to_all(wanted, "dp", split_axis=0, concat_axis=0, tiled=True)
    anchors_here = lax.all_to_all(anchors, "dp", split_axis=0, concat_axis=0, tiled=True)
    partners = descriptors.at[jnp.maximum(wanted_here, 0).reshape(-1)].get(
        mode="promise_in_bounds"
    )
    slots = peer_count * slot_count
    live = jnp.broadcast_to((wanted_here.reshape(slots, 1) >= 0).astype(F32), (slots, NB))
    packed = gram(
        1.0 / pairs_all,
        shrink_weight / rows_all,
        anchors_here.reshape(slots, feature_width),
        partners,
        live,
        descriptors,
    )
    inverse, col_mean = inverse_factor(reduce_all(packed))
    return whiten(database, col_mean, inverse)


def solution(mesh):
    placed = (
        P(("dp", "mp"), None),
        P(("dp", "mp"), None),
        P(("dp", "mp"), None, None),
        P(("dp", "mp"), None, None),
        P(("dp", "mp"), None),
    )
    return jax.shard_map(
        shards, mesh=mesh, in_specs=placed, out_specs=P(("dp", "mp"), None), check_vma=False
    )
```

```python
import functools

import jax
import jax.numpy as jnp
from jax import lax
from jax.experimental import pallas as pl
from jax.experimental.pallas import tpu as pltpu
from jax.sharding import PartitionSpec as P

PAIRS_DEV = 1024
R_ALL = 262144


shrink_weight = 0.5
ridge_term = 0.05
norm_epsilon = 1e-06
contract_rows = (((0,), (0,)), ((), ()))

N = 1024
NB = 128
F32 = jnp.float32
HI = lax.Precision.HIGHEST

def lane_bcast(x, c):
    return jnp.broadcast_to(x[:, c:c + 1], x.shape)

def row_bcast(x, i):
    return jnp.broadcast_to(x[i:i + 1, :], x.shape)

def factor_block(rows):
    lane = lax.broadcasted_iota(jnp.int32, (8, NB), 1)
    count = len(rows)
    for q in range(count):
        base = 8 * q
        inside = (lane >= base) & (lane < base + 8)
        cur = rows[q]
        cols = [lane_bcast(cur, base + j) for j in range(8)]
        d = {}
        for j in range(8):
            for i in range(j, 8):
                d[i, j] = row_bcast(cols[j], i)
        w = [jnp.where(inside, jnp.where(lane == base + i, 1.0, 0.0), row_bcast(cur, i)) for i in range(8)]
        inv, l, rs = [], {}, []
        for j in range(8):
            p = d[j, j]
            r = 1.0 / p
            inv.append(r)
            rs.append(lax.rsqrt(p))
            for i in range(j + 1, 8):
                l[i, j] = d[i, j] * r
            for i in range(j + 1, 8):
                for k in range(j + 1, i + 1):
                    d[i, k] = d[i, k] - l[i, j] * d[k, j]
            for i in range(j + 1, 8):
                w[i] = w[i] - l[i, j] * w[j]
        g = [None] * 8
        for i in range(7, -1, -1):
            acc = inv[i] * w[i]
            for j in range(i + 1, 8):
                acc = acc - l[j, i] * g[j]
            g[i] = acc
        sub = lax.broadcasted_iota(jnp.int32, (8, NB), 0)
        out = rs[0] * w[0]
        for i in range(1, 8):
            out = jnp.where(sub == i, rs[i] * w[i], out)
        rows[q] = out
        for t in range(q + 1, count):
            acc = jnp.where(inside, 0.0, rows[t])
            for j in range(8):
                acc = acc - lane_bcast(rows[t], base + j) * g[j]
            rows[t] = acc
    return rows


NX, NY, NZ, NC = 4, 4, 8, 2
PLANE = NX * NY
BLOCKS = N // NB
UPPER = [(i, j) for i in range(BLOCKS) for j in range(i, BLOCKS)]
DATA = len(UPPER) * NB // (NC * PLANE)
UNIT = DATA + 8
HALF = PLANE * UNIT
PIECE = 24
SEG = 16


def segments():
    found = []
    for b, (i, j) in enumerate(UPPER):
        for s in range(0, NB, SEG):
            flat = b * NB + s
            unit, inside = flat // DATA, flat % DATA
            found.append((i, j, s, unit * UNIT + inside))
    return found


MESH = pl.DeviceIdType.MESH
CAP = 24
GROUP = NZ * NC
PEERS = NX * GROUP


def one_hot_rows(index, count):
    lane = lax.broadcasted_iota(jnp.int32, (count, NB), 1).astype(F32)
    parts = [jnp.where(index == lane + float(NB * c), 1.0, 0.0).astype(jnp.bfloat16) for c in range(N // NB)]
    return jnp.concatenate(parts, axis=1)


def pairs_kernel(pair_scale, row_scale, anchor_ref, wanted_ref, desc_ref, out_ref,
                 sbuf, rbuf, windex, wcol, part_ref, diff_ref, gram_ref, s0, q0, s1, q1):
    dp, y = lax.axis_index("dp"), lax.axis_index("mp")
    core, z, x = dp % NC, (dp // NC) % NZ, dp // (NC * NZ)

    def peer(ox, o):
        return ((x + ox) % NX) * GROUP + ((z + o // NC) % NZ) * NC + (core + o % NC) % NC

    def peer_from(ox, o):
        return ((x + NX - ox) % NX) * GROUP + ((z + NZ - o // NC) % NZ) * NC + (core + NC - o % NC) % NC

    def copy_rows(slot, target, owner):
        return pltpu.make_async_remote_copy(
            src_ref=sbuf.at[target], dst_ref=rbuf.at[owner], send_sem=s0.at[slot], recv_sem=q0.at[slot],
            device_id=(target, y), device_id_type=MESH,
        )

    def copy_index(slot, target, owner):
        return pltpu.make_async_remote_copy(
            src_ref=wanted_ref.at[target], dst_ref=windex.at[owner], send_sem=s1.at[slot], recv_sem=q1.at[slot],
            device_id=(target, y), device_id_type=MESH,
        )

    barrier = pltpu.get_barrier_semaphore()

    @pl.loop(1, PEERS)
    def _(k):
        pl.semaphore_signal(barrier, inc=1, device_id=(peer(k // GROUP, k % GROUP), y), device_id_type=MESH)

    rows_x = GROUP * CAP

    def gather(ox):
        group = (x + ox) % NX
        base = group * rows_x
        for h in range(2):
            count = rows_x // 2
            index = anchor_ref[pl.ds(pl.multiple_of(base + h * count, count), count), :]
            found = jnp.dot(one_hot_rows(index, count), desc_ref[...], preferred_element_type=F32)
            for p in range(GROUP // 2):
                block = found[p * CAP:(p + 1) * CAP, :]
                block = jnp.concatenate([block[:, :N // 2], block[:, N // 2:]], axis=0)
                sbuf[group * GROUP + h * (GROUP // 2) + p] = block.astype(jnp.bfloat16)

    gather(0)
    pl.semaphore_wait(barrier, PEERS - 1)

    @pl.loop(0, NX)
    def _(ox):
        @pl.loop(0, GROUP)
        def _(o):
            slot = ox * GROUP + o

            @pl.when(slot > 0)
            def _():
                copy_rows(slot, peer(ox, o), dp).start()

        @pl.when(ox == 0)
        def _():
            @pl.loop(1, PEERS)
            def _(k):
                copy_index(k, peer(k // GROUP, k % GROUP), dp).start()

        @pl.when(ox < NX - 1)
        def _():
            gather(ox + 1)

    tile = 256
    for i in range(0, N, tile):
        gram_ref[i:i + tile, i:] = row_scale * lax.dot_general(
            desc_ref[:, i:i + tile], desc_ref[:, i:], contract_rows, preferred_element_type=F32)
    ones = jnp.ones((8, desc_ref.shape[0]), jnp.bfloat16)
    sums = jnp.dot(ones, desc_ref[...], preferred_element_type=F32)
    sub = lax.broadcasted_iota(jnp.int32, (8, NB), 0)
    packed = sums[:, 0:NB]
    for i in range(1, BLOCKS):
        packed = jnp.where(sub == i, sums[:, i * NB:(i + 1) * NB], packed)
    for u in range(NC * PLANE):
        out_ref[u * UNIT + DATA:(u + 1) * UNIT, :] = packed

    windex[dp] = wanted_ref[dp]

    @pl.loop(1, PEERS)
    def _(k):
        copy_index(k, peer(k // GROUP, k % GROUP), peer_from(k // GROUP, k % GROUP)).wait_recv()

    turned = windex[...].reshape(PEERS, NB)
    turned = jnp.concatenate([turned, jnp.zeros((NB - PEERS, NB), F32)], axis=0).T
    for p in range(PEERS):
        wcol[p * CAP:(p + 1) * CAP, :] = jnp.broadcast_to(turned[0:CAP, p:p + 1], (CAP, NB))

    count = 192

    @pl.loop(0, PEERS * CAP // count)
    def _(g):
        at = pl.ds(pl.multiple_of(g * count, count), count)
        found = jnp.dot(one_hot_rows(wcol[at, :], count), desc_ref[...], preferred_element_type=F32)
        part_ref[at, :] = found.astype(jnp.bfloat16)

    rbuf[dp] = sbuf[dp]

    @pl.loop(0, NX)
    def _(ox):
        group = (x + NX - ox) % NX

        @pl.loop(0, GROUP)
        def _(o):
            slot = ox * GROUP + o

            @pl.when(slot > 0)
            def _():
                copy_rows(slot, peer(ox, o), peer_from(ox, o)).wait_recv()

        @pl.loop(0, GROUP // 2)
        def _(m):
            first = group * GROUP + 2 * m
            blocks = []
            for e in range(2):
                got = rbuf[first + e].astype(F32)
                blocks.append(jnp.concatenate([got[:CAP], got[CAP:]], axis=1))
            at = pl.multiple_of(first * CAP, 2 * CAP)
            gap = jnp.concatenate(blocks, axis=0) - part_ref[pl.ds(at, 2 * CAP), :].astype(F32)
            diff_ref[pl.ds(pl.multiple_of(m * 2 * CAP, 2 * CAP), 2 * CAP), :] = gap.astype(jnp.bfloat16)

        for i in range(0, N, tile):
            gram_ref[i:i + tile, i:] = gram_ref[i:i + tile, i:] + pair_scale * lax.dot_general(
                diff_ref[:, i:i + tile], diff_ref[:, i:], contract_rows, preferred_element_type=F32)

    for i, j, s, at in segments():
        out_ref[at:at + SEG, :] = gram_ref[i * NB + s:i * NB + s + SEG, j * NB:(j + 1) * NB]

    @pl.loop(1, PEERS)
    def _(k):
        copy_rows(k, peer(k // GROUP, k % GROUP), dp).wait_send()
        copy_index(k, peer(k // GROUP, k % GROUP), dp).wait_send()


def pair_grams(pair_scale, row_scale, anchor, wanted, descriptors):
    dma = pltpu.SemaphoreType.DMA
    return pl.pallas_call(
        functools.partial(pairs_kernel, pair_scale, row_scale),
        out_shape=jax.ShapeDtypeStruct((NC * HALF, NB), F32),
        in_specs=[pl.BlockSpec(memory_space=pltpu.VMEM)] * 3,
        out_specs=pl.BlockSpec(memory_space=pltpu.VMEM),
        scratch_shapes=[
            pltpu.VMEM((PEERS, 2 * CAP, N // 2), jnp.bfloat16),
            pltpu.VMEM((PEERS, 2 * CAP, N // 2), jnp.bfloat16),
            pltpu.VMEM((PEERS, 1, NB), F32),
            pltpu.VMEM((PEERS * CAP, NB), F32),
            pltpu.VMEM((PEERS * CAP, N), jnp.bfloat16),
            pltpu.VMEM((GROUP * CAP, N), jnp.bfloat16),
            pltpu.VMEM((N, N), F32),
        ] + [dma((PEERS,))] * 4,
        compiler_params=pltpu.CompilerParams(
            collective_id=2, has_side_effects=True, vmem_limit_bytes=48 << 20
        ),
    )(anchor, wanted, descriptors)


def reduce_kernel(p_ref, out_ref, half, r0, r1, zb, r2, gz, s0, q0, s1, q1, s2, q2, s3, q3, s4, q4, s5, q5):
    dp, y = lax.axis_index("dp"), lax.axis_index("mp")
    core, z, x = dp % NC, (dp // NC) % NZ, dp // (NC * NZ)
    sibling = (dp + 1 - 2 * core, y)
    mine = x * NY + y

    def plane(o):
        return (x + o // NY) % NX, (y + o % NY) % NY

    def plane_from(o):
        return (x + NX - o // NY) % NX, (y + NY - o % NY) % NY

    def plane_id(o):
        tx, ty = plane(o)
        return ((tx * NZ + z) * NC + core, ty)

    def line_id(o):
        return ((x * NZ + (z + o) % NZ) * NC + core, y)

    def rows(base, count):
        return pl.ds(pl.multiple_of(base, 8), count)

    def send(src, dst, ssem, rsem, target):
        return pltpu.make_async_remote_copy(
            src_ref=src, dst_ref=dst, send_sem=ssem, recv_sem=rsem,
            device_id=target, device_id_type=pl.DeviceIdType.MESH,
        )

    barrier = pltpu.get_barrier_semaphore()
    pl.semaphore_signal(barrier, inc=1, device_id=sibling, device_id_type=pl.DeviceIdType.MESH)

    @pl.loop(1, PLANE)
    def _(o):
        pl.semaphore_signal(barrier, inc=1, device_id=plane_id(o), device_id_type=pl.DeviceIdType.MESH)

    @pl.loop(1, NZ)
    def _(o):
        pl.semaphore_signal(barrier, inc=1, device_id=line_id(o), device_id_type=pl.DeviceIdType.MESH)

    pl.semaphore_wait(barrier, 1 + (PLANE - 1) + (NZ - 1))

    def unit_at(o):
        tx, ty = plane(o)
        return (tx * NY + ty) * UNIT

    def copy0(o):
        at = unit_at(o)
        return send(p_ref.at[rows((1 - core) * HALF + at, UNIT)], r0.at[rows(at, UNIT)], s0.at[o], q0.at[o], sibling)

    def copy1(o):
        return send(half.at[rows(unit_at(o), UNIT)], r1.at[o], s1.at[o], q1.at[o], plane_id(o))

    @pl.loop(0, PLANE)
    def _(i):
        copy0((i + 1) % PLANE).start()

    zb[UNIT:, :] = jnp.zeros((zb.shape[0] - UNIT, NB), F32)

    @pl.loop(1, PLANE)
    def _(o):
        copy0(o).wait_recv()
        at = unit_at(o)
        half[rows(at, UNIT), :] = p_ref[rows(core * HALF + at, UNIT), :] + r0[rows(at, UNIT), :]
        copy1(o).start()

    copy0(0).wait_recv()
    at = mine * UNIT
    zb[0:UNIT, :] = p_ref[rows(core * HALF + at, UNIT), :] + r0[rows(at, UNIT), :]

    @pl.loop(1, PLANE)
    def _(o):
        copy1(o).wait_recv()
        zb[0:UNIT, :] = zb[0:UNIT, :] + r1[o]

    def copy2(o):
        return send(zb.at[rows(((z + o) % NZ) * PIECE, PIECE)], r2.at[o], s2.at[o], q2.at[o], line_id(o))

    def copy3(o, owner):
        piece = gz.at[rows(owner * PIECE, PIECE)]
        return send(piece, piece, s3.at[o], q3.at[o], line_id(o))

    @pl.loop(1, NZ)
    def _(o):
        copy2(o).start()

    own = rows(z * PIECE, PIECE)
    gz[own, :] = zb[own, :]

    @pl.loop(1, NZ)
    def _(o):
        copy2(o).wait_recv()
        gz[own, :] = gz[own, :] + r2[o]

    @pl.loop(1, NZ)
    def _(o):
        copy3(o, z).start()

    @pl.loop(1, NZ)
    def _(o):
        copy3(o, (z + NZ - o) % NZ).wait_recv()

    def copy4(o, unit):
        return send(gz.at[pl.ds(0, UNIT)], out_ref.at[rows(core * HALF + unit * UNIT, UNIT)], s4.at[o], q4.at[o], plane_id(o))

    def copy5(o, which):
        tx, ty = plane_from(o)
        piece = out_ref.at[rows(which * HALF + (tx * NY + ty) * UNIT, UNIT)]
        return send(piece, piece, s5.at[o], q5.at[o], sibling)

    @pl.loop(1, PLANE)
    def _(o):
        copy4(o, mine).start()

    out_ref[rows(core * HALF + mine * UNIT, UNIT), :] = gz[0:UNIT, :]
    copy5(0, core).start()

    @pl.loop(1, PLANE)
    def _(o):
        tx, ty = plane_from(o)
        copy4(o, tx * NY + ty).wait_recv()
        copy5(o, core).start()

    @pl.loop(0, PLANE)
    def _(o):
        copy5(o, 1 - core).wait_recv()
        copy5(o, core).wait_send()
        copy0(o).wait_send()

    @pl.loop(1, PLANE)
    def _(o):
        copy1(o).wait_send()
        copy4(o, mine).wait_send()

    @pl.loop(1, NZ)
    def _(o):
        copy2(o).wait_send()
        copy3(o, z).wait_send()


def reduce_all(packed):
    dma = pltpu.SemaphoreType.DMA
    return pl.pallas_call(
        reduce_kernel,
        out_shape=jax.ShapeDtypeStruct((NC * HALF, NB), F32),
        in_specs=[pl.BlockSpec(memory_space=pltpu.VMEM)],
        out_specs=pl.BlockSpec(memory_space=pltpu.VMEM),
        scratch_shapes=[
            pltpu.VMEM((HALF, NB), F32),
            pltpu.VMEM((HALF, NB), F32),
            pltpu.VMEM((PLANE, UNIT, NB), F32),
            pltpu.VMEM((NZ * PIECE, NB), F32),
            pltpu.VMEM((NZ, PIECE, NB), F32),
            pltpu.VMEM((NZ * PIECE, NB), F32),
        ] + [dma((PLANE,))] * 4 + [dma((NZ,))] * 4 + [dma((PLANE,))] * 4,
        compiler_params=pltpu.CompilerParams(
            collective_id=1, has_side_effects=True, vmem_limit_bytes=40 << 20
        ),
    )(packed)


def chol_kernel(p_ref, out_ref, mean_ref, c_ref, t_ref):
    rows_all = R_ALL
    c_ref[...] = jnp.zeros((N, N), F32)
    mean_ref[...] = jnp.zeros((8, N), F32)
    means = p_ref[DATA:UNIT, :] * (1.0 / rows_all)
    for i in range(BLOCKS):
        mean_ref[0:1, i * NB:(i + 1) * NB] = means[i:i + 1, :]
    for i, j, s, at in segments():
        c_ref[i * NB + s:i * NB + s + SEG, j * NB:(j + 1) * NB] = p_ref[at:at + SEG, :]
    row = lax.broadcasted_iota(jnp.int32, (NB, NB), 0)
    col = lax.broadcasted_iota(jnp.int32, (NB, NB), 1)
    for i in range(BLOCKS):
        a = i * NB
        outer = lax.dot_general(mean_ref[:, a:a + NB], mean_ref[:, a:], contract_rows,
                                precision=HI, preferred_element_type=F32)
        c_ref[a:a + NB, a:] = c_ref[a:a + NB, a:] - shrink_weight * outer
        c_ref[a:a + NB, a:a + NB] = c_ref[a:a + NB, a:a + NB] + jnp.where(row == col, ridge_term, 0.0)
    blocks = BLOCKS

    def step(k, _):
        off = pl.multiple_of(k * NB, NB)
        diag = c_ref.at[pl.ds(off, NB), pl.ds(off, NB)]
        rows = [diag[8 * q:8 * q + 8, :] for q in range(16)]
        rows = factor_block(rows)
        for q in range(16):
            t_ref[8 * q:8 * q + 8, :] = rows[q]
        t = jnp.where(row >= col, t_ref[...], 0.0)
        ck = jnp.dot(t, c_ref[pl.ds(off, NB), :], precision=HI, preferred_element_type=F32)
        c_ref[pl.ds(off, NB), :] = ck
        c_ref[pl.ds(off, NB), pl.ds(off, NB)] = t

        def update(i, _):
            io = pl.multiple_of(i * NB, NB)
            u = c_ref[pl.ds(off, NB), pl.ds(io, NB)]
            c_ref[pl.ds(io, NB), pl.ds(off, NB)] = jnp.zeros((NB, NB), F32)
            prod = lax.dot_general(u, c_ref[pl.ds(off, NB), :], (((0,), (0,)), ((), ())),
                                   precision=HI, preferred_element_type=F32)
            c_ref[pl.ds(io, NB), :] = c_ref[pl.ds(io, NB), :] - prod
            return 0
        lax.fori_loop(k + 1, blocks, update, 0)
        return 0
    lax.fori_loop(0, blocks, step, 0)
    for i in range(blocks):
        r = lax.broadcasted_iota(jnp.int32, (NB, N), 0) + i * NB
        c = lax.broadcasted_iota(jnp.int32, (NB, N), 1)
        out_ref[i * NB:(i + 1) * NB, :] = jnp.where(r >= c, c_ref[i * NB:(i + 1) * NB, :], 0.0).astype(out_ref.dtype)


def inverse_factor(packed):
    return pl.pallas_call(
        chol_kernel,
        out_shape=[jax.ShapeDtypeStruct((N, N), jnp.bfloat16), jax.ShapeDtypeStruct((8, N), F32)],
        in_specs=[pl.BlockSpec(memory_space=pltpu.VMEM)],
        out_specs=[pl.BlockSpec(memory_space=pltpu.VMEM)] * 2,
        scratch_shapes=[pltpu.VMEM((N, N), F32), pltpu.VMEM((NB, NB), F32)],
        compiler_params=pltpu.CompilerParams(vmem_limit_bytes=40 << 20),
    )(packed)


def whiten_kernel(db_ref, mean_ref, inv_ref, out_ref):
    centered = (db_ref[...].astype(F32) - mean_ref[0:1, :]).astype(jnp.bfloat16)
    projected = lax.dot_general(
        centered, inv_ref[...], (((1,), (1,)), ((), ())), preferred_element_type=F32
    )
    energy = jnp.mean(projected * projected, axis=1, keepdims=True)
    out_ref[...] = (projected * lax.rsqrt(energy + norm_epsilon)).astype(jnp.bfloat16)


def whiten(database, col_mean, inverse):
    rows, width = database.shape
    tile = 256
    return pl.pallas_call(
        whiten_kernel,
        grid=(rows // tile,),
        out_shape=jax.ShapeDtypeStruct((rows, width), jnp.bfloat16),
        in_specs=[
            pl.BlockSpec((tile, width), lambda i: (i, 0)),
            pl.BlockSpec((8, width), lambda i: (0, 0)),
            pl.BlockSpec((width, width), lambda i: (0, 0)),
        ],
        out_specs=pl.BlockSpec((tile, width), lambda i: (i, 0)),
        compiler_params=pltpu.CompilerParams(vmem_limit_bytes=40 << 20),
    )(database, col_mean, inverse)


def shards(descriptors, database, anchor_row, partner_row, block_counts):
    local_rows = descriptors.shape[0]
    peer_count = partner_row.shape[1]
    slot_count = partner_row.shape[2]
    devices = lax.axis_size("dp") * lax.axis_size("mp")
    pairs_all = PAIRS_DEV * devices
    rows_all = local_rows * devices
    slot_iota = lax.broadcasted_iota(jnp.int32, (peer_count, slot_count), 1)
    live_slots = slot_iota < block_counts[0][:, None]
    wanted = jnp.where(live_slots, partner_row[0], -1).astype(F32)
    wanted = jnp.pad(wanted, ((0, 0), (0, NB - slot_count)))[:, None, :]
    anchor = jnp.where(live_slots, anchor_row[0], -1).astype(F32).reshape(-1, 1)
    packed = pair_grams(
        1.0 / pairs_all,
        shrink_weight / rows_all,
        jnp.broadcast_to(anchor, (peer_count * slot_count, NB)),
        wanted,
        descriptors,
    )
    inverse, col_mean = inverse_factor(reduce_all(packed))
    return whiten(database, col_mean, inverse)


def solution(mesh):
    placed = (
        P(("dp", "mp"), None),
        P(("dp", "mp"), None),
        P(("dp", "mp"), None, None),
        P(("dp", "mp"), None, None),
        P(("dp", "mp"), None),
    )
    return jax.shard_map(
        shards, mesh=mesh, in_specs=placed, out_specs=P(("dp", "mp"), None), check_vma=False
    )
```

```python
import functools

import jax
import jax.numpy as jnp
from jax import lax
from jax.experimental import pallas as pl
from jax.experimental.pallas import tpu as pltpu
from jax.sharding import PartitionSpec as P

PAIRS_DEV = 1024


shrink_weight = 0.5
ridge_term = 0.05
norm_epsilon = 1e-06
contract_rows = (((0,), (0,)), ((), ()))

N = 1024
NB = 128
F32 = jnp.float32
HI = lax.Precision.HIGHEST
MESH = pl.DeviceIdType.MESH

def lane_bcast(x, c):
    return jnp.take_along_axis(x, jnp.full(x.shape, c, jnp.int32), axis=1, mode="promise_in_bounds")


def row_bcast(x, i):
    return jnp.broadcast_to(x[i:i + 1, :], x.shape)


def factor_block(rows):
    lane = lax.broadcasted_iota(jnp.int32, (8, NB), 1)
    sub = lax.broadcasted_iota(jnp.int32, (8, NB), 0)
    count = len(rows)
    for q in range(count):
        base = 8 * q
        inside = (lane >= base) & (lane < base + 8)
        own = [row_bcast(rows[q], i) for i in range(8)]
        d = {}
        for j in range(8):
            for i in range(j, 8):
                d[i, j] = lane_bcast(own[i], base + j)
        w = [jnp.where(inside, jnp.where(lane == base + i, 1.0, 0.0), own[i]) for i in range(8)]
        ahead = q + 1 < count
        v = [lane_bcast(rows[q + 1], base + j) for j in range(8)] if ahead else None
        inv, scale, low = [], [], {}
        for j in range(8):
            s = lax.rsqrt(d[j, j])
            r = s * s
            inv.append(r)
            scale.append(s)
            for i in range(j + 1, 8):
                low[i, j] = d[i, j] * r
            for i in range(j + 1, 8):
                for k in range(j + 1, i + 1):
                    d[i, k] = d[i, k] - low[i, j] * d[k, j]
            for i in range(j + 1, 8):
                w[i] = w[i] - low[i, j] * w[j]
                if ahead:
                    v[i] = v[i] - low[i, j] * v[j]
        if ahead:
            following = jnp.where(inside, 0.0, rows[q + 1])
            for j in range(8):
                following = following - v[j] * (inv[j] * w[j])
        g = [None] * 8
        for i in range(7, -1, -1):
            acc = inv[i] * w[i]
            for j in range(i + 1, 8):
                acc = acc - low[j, i] * g[j]
            g[i] = acc
        out = scale[0] * w[0]
        for i in range(1, 8):
            out = jnp.where(sub == i, scale[i] * w[i], out)
        rows[q] = out
        for t in range(q + 2, count):
            acc = jnp.where(inside, 0.0, rows[t])
            for j in range(8):
                acc = acc - lane_bcast(rows[t], base + j) * g[j]
            rows[t] = acc
        if ahead:
            rows[q + 1] = following
    return rows


NX, NY, NZ, NC = 4, 4, 8, 2
PLANE = NX * NY
BLOCKS = N // NB
CAP = 24
GROUP = NZ * NC
PEERS = NX * GROUP
CUT = N // 2
LEFT = [(i, j) for j in range(BLOCKS // 2) for i in range(j + 1)]
RIGHT = [(i, j) for j in range(BLOCKS // 2, BLOCKS) for i in range(j + 1)]
DATA_LEFT = len(LEFT) * NB // (NC * PLANE)
UNIT_LEFT = DATA_LEFT + 8
UNIT_RIGHT = len(RIGHT) * NB // (NC * PLANE)
PIECE_LEFT, PIECE_RIGHT = 8, 16


def segments(blocks, data, unit):
    found = []
    for b, (i, j) in enumerate(blocks):
        for s in range(0, NB, 8):
            flat = b * NB + s
            found.append((i * NB + s, j * NB, flat // data * unit + flat % data))
    return found


def one_hot_rows(index, count):
    lane = lax.broadcasted_iota(jnp.int32, (count, NB), 1).astype(F32)
    parts = [jnp.where(index == lane + float(NB * c), 1.0, 0.0).astype(jnp.bfloat16) for c in range(N // NB)]
    return jnp.concatenate(parts, axis=1)


def rows_at(base, count):
    return pl.ds(pl.multiple_of(base, 8), count)


class Sum:
    def __init__(self, unit, piece, p_ref, out_ref, half, r0, r1, zb, r2, gz, near, far):
        self.unit, self.piece, self.half_rows = unit, piece, PLANE * unit
        self.p, self.out, self.half, self.r0, self.r1 = p_ref, out_ref, half, r0, r1
        self.zb, self.r2, self.gz, self.near, self.far = zb, r2, gz, near, far
        dp, self.y = lax.axis_index("dp"), lax.axis_index("mp")
        self.core, self.z, self.x = dp % NC, (dp // NC) % NZ, dp // (NC * NZ)
        self.sibling = (dp + 1 - 2 * self.core, self.y)
        self.mine = self.x * NY + self.y

    def plane(self, o):
        return (self.x + o // NY) % NX, (self.y + o % NY) % NY

    def plane_from(self, o):
        return (self.x + NX - o // NY) % NX, (self.y + NY - o % NY) % NY

    def plane_id(self, o):
        tx, ty = self.plane(o)
        return ((tx * NZ + self.z) * NC + self.core, ty)

    def line_id(self, o):
        return ((self.x * NZ + (self.z + o) % NZ) * NC + self.core, self.y)

    def near_copy(self, pair, o, src, dst, target):
        return pltpu.make_async_remote_copy(
            src_ref=src, dst_ref=dst, send_sem=self.near.at[2 * pair, o], recv_sem=self.near.at[2 * pair + 1, o],
            device_id=target, device_id_type=MESH)

    def far_copy(self, pair, o, src, dst, target):
        return pltpu.make_async_remote_copy(
            src_ref=src, dst_ref=dst, send_sem=self.far.at[2 * pair, o], recv_sem=self.far.at[2 * pair + 1, o],
            device_id=target, device_id_type=MESH)

    def unit_at(self, o):
        tx, ty = self.plane(o)
        return (tx * NY + ty) * self.unit

    def copy0(self, o):
        at = self.unit_at(o)
        src = self.p.at[rows_at((1 - self.core) * self.half_rows + at, self.unit)]
        return self.near_copy(0, o, src, self.r0.at[rows_at(at, self.unit)], self.sibling)

    def copy1(self, o):
        return self.near_copy(1, o, self.half.at[rows_at(self.unit_at(o), self.unit)], self.r1.at[o], self.plane_id(o))

    def copy2(self, o):
        src = self.zb.at[rows_at(((self.z + o) % NZ) * self.piece, self.piece)]
        return self.far_copy(0, o, src, self.r2.at[o], self.line_id(o))

    def copy3(self, o, owner):
        part = self.gz.at[rows_at(owner * self.piece, self.piece)]
        return self.far_copy(1, o, part, part, self.line_id(o))

    def copy4(self, o, owner):
        dst = self.out.at[rows_at(self.core * self.half_rows + owner * self.unit, self.unit)]
        return self.near_copy(2, o, self.gz.at[pl.ds(0, self.unit)], dst, self.plane_id(o))

    def copy5(self, o, which):
        tx, ty = self.plane_from(o)
        part = self.out.at[rows_at(which * self.half_rows + (tx * NY + ty) * self.unit, self.unit)]
        return self.near_copy(3, o, part, part, self.sibling)

    def to_sibling(self):
        @pl.loop(0, PLANE)
        def _(i):
            self.copy0((i + 1) % PLANE).start()

        pad = self.zb.shape[0] - self.unit
        self.zb[self.unit:, :] = jnp.zeros((pad, NB), F32)

    def to_plane(self):
        @pl.loop(1, PLANE)
        def _(o):
            self.copy0(o).wait_recv()
            at = self.unit_at(o)
            own = self.p[rows_at(self.core * self.half_rows + at, self.unit), :]
            self.half[rows_at(at, self.unit), :] = own + self.r0[rows_at(at, self.unit), :]
            self.copy1(o).start()

        self.copy0(0).wait_recv()
        at = self.mine * self.unit
        own = self.p[rows_at(self.core * self.half_rows + at, self.unit), :]
        self.zb[0:self.unit, :] = own + self.r0[rows_at(at, self.unit), :]

    def to_line(self):
        @pl.loop(1, PLANE)
        def _(o):
            self.copy1(o).wait_recv()
            self.zb[0:self.unit, :] = self.zb[0:self.unit, :] + self.r1[o]

        @pl.loop(1, NZ)
        def _(o):
            self.copy2(o).start()

        own = rows_at(self.z * self.piece, self.piece)
        self.gz[own, :] = self.zb[own, :]

        @pl.loop(1, NZ)
        def _(o):
            self.copy2(o).wait_recv()
            self.gz[own, :] = self.gz[own, :] + self.r2[o]

        @pl.loop(1, NZ)
        def _(o):
            self.copy3(o, self.z).start()

        @pl.loop(1, NZ)
        def _(o):
            self.copy3(o, (self.z + NZ - o) % NZ).wait_recv()

        @pl.loop(1, PLANE)
        def _(o):
            self.copy4(o, self.mine).start()

        self.out[rows_at(self.core * self.half_rows + self.mine * self.unit, self.unit), :] = self.gz[0:self.unit, :]
        self.copy5(0, self.core).start()

    def finish(self):
        @pl.loop(1, PLANE)
        def _(o):
            tx, ty = self.plane_from(o)
            self.copy4(o, tx * NY + ty).wait_recv()
            self.copy5(o, self.core).start()

        @pl.loop(0, PLANE)
        def _(o):
            self.copy5(o, 1 - self.core).wait_recv()
            self.copy5(o, self.core).wait_send()
            self.copy0(o).wait_send()

        @pl.loop(1, PLANE)
        def _(o):
            self.copy1(o).wait_send()
            self.copy4(o, self.mine).wait_send()

        @pl.loop(1, NZ)
        def _(o):
            self.copy2(o).wait_send()
            self.copy3(o, self.z).wait_send()


def factor_kernel(pair_scale, row_scale, rows_all, anchor_ref, wanted_ref, desc_ref, out_ref, mean_ref,
                  sbuf, rbuf, windex, wcol, part_ref, diff_ref, gram_ref, c_ref, t_ref, s0, q0, s1, q1,
                  *sums):
    dp, y = lax.axis_index("dp"), lax.axis_index("mp")
    core, z, x = dp % NC, (dp // NC) % NZ, dp // (NC * NZ)
    left = Sum(UNIT_LEFT, PIECE_LEFT, *sums[:10])
    right = Sum(UNIT_RIGHT, PIECE_RIGHT, *sums[10:])

    def peer(ox, o):
        return ((x + ox) % NX) * GROUP + ((z + o // NC) % NZ) * NC + (core + o % NC) % NC

    def peer_from(ox, o):
        return ((x + NX - ox) % NX) * GROUP + ((z + NZ - o // NC) % NZ) * NC + (core + NC - o % NC) % NC

    def copy_rows(part, slot, target, owner):
        return pltpu.make_async_remote_copy(
            src_ref=sbuf.at[part, target], dst_ref=rbuf.at[part, owner], send_sem=s0.at[part, slot],
            recv_sem=q0.at[part, slot], device_id=(target, y), device_id_type=MESH)

    def copy_index(slot, target, owner):
        return pltpu.make_async_remote_copy(
            src_ref=wanted_ref.at[target], dst_ref=windex.at[owner], send_sem=s1.at[slot], recv_sem=q1.at[slot],
            device_id=(target, y), device_id_type=MESH)

    barrier = pltpu.get_barrier_semaphore()

    @pl.loop(1, PEERS)
    def _(k):
        pl.semaphore_signal(barrier, inc=1, device_id=(peer(k // GROUP, k % GROUP), y), device_id_type=MESH)

    @pl.loop(1, PLANE)
    def _(o):
        @pl.when(o % NY != 0)
        def _():
            pl.semaphore_signal(barrier, inc=1, device_id=left.plane_id(o), device_id_type=MESH)

    rows_x = GROUP * CAP

    def gather(ox):
        group = (x + ox) % NX
        base = group * rows_x
        for h in range(2):
            count = rows_x // 2
            index = anchor_ref[pl.ds(pl.multiple_of(base + h * count, count), count), :]
            found = jnp.dot(one_hot_rows(index, count), desc_ref[...], preferred_element_type=F32)
            for p in range(GROUP // 2):
                block = found[p * CAP:(p + 1) * CAP, :]
                for part in range(2):
                    a = part * CUT
                    halves = jnp.concatenate([block[:, a:a + CUT // 2], block[:, a + CUT // 2:a + CUT]], axis=0)
                    sbuf[part, group * GROUP + h * (GROUP // 2) + p] = halves.astype(jnp.bfloat16)

    gather(0)
    pl.semaphore_wait(barrier, PEERS - 1 + PLANE - NX)

    @pl.loop(0, NX)
    def _(ox):
        @pl.loop(0, GROUP)
        def _(o):
            slot = ox * GROUP + o

            @pl.when(slot > 0)
            def _():
                copy_rows(0, slot, peer(ox, o), dp).start()

        @pl.when(ox == 0)
        def _():
            @pl.loop(1, PEERS)
            def _(k):
                copy_index(k, peer(k // GROUP, k % GROUP), dp).start()

        @pl.when(ox < NX - 1)
        def _():
            gather(ox + 1)

    @pl.loop(1, PEERS)
    def _(k):
        copy_rows(1, k, peer(k // GROUP, k % GROUP), dp).start()

    tile = 256
    for i in range(0, N, tile):
        gram_ref[i:i + tile, i:] = row_scale * lax.dot_general(
            desc_ref[:, i:i + tile], desc_ref[:, i:], contract_rows, preferred_element_type=F32)
    ones = jnp.ones((8, desc_ref.shape[0]), jnp.bfloat16)
    sums_row = jnp.dot(ones, desc_ref[...], preferred_element_type=F32)
    sub = lax.broadcasted_iota(jnp.int32, (8, NB), 0)
    packed = sums_row[:, 0:NB]
    for i in range(1, BLOCKS):
        packed = jnp.where(sub == i, sums_row[:, i * NB:(i + 1) * NB], packed)
    for u in range(NC * PLANE):
        left.p[u * UNIT_LEFT + DATA_LEFT:(u + 1) * UNIT_LEFT, :] = packed

    windex[dp] = wanted_ref[dp]

    @pl.loop(1, PEERS)
    def _(k):
        copy_index(k, peer(k // GROUP, k % GROUP), peer_from(k // GROUP, k % GROUP)).wait_recv()

    turned = windex[...].reshape(PEERS, NB)
    turned = jnp.concatenate([turned, jnp.zeros((NB - PEERS, NB), F32)], axis=0).T
    for p in range(PEERS):
        wcol[p * CAP:(p + 1) * CAP, :] = jnp.broadcast_to(turned[0:CAP, p:p + 1], (CAP, NB))

    count = 192

    @pl.loop(0, PEERS * CAP // count)
    def _(g):
        at = pl.ds(pl.multiple_of(g * count, count), count)
        found = jnp.dot(one_hot_rows(wcol[at, :], count), desc_ref[...], preferred_element_type=F32)
        part_ref[at, :] = found.astype(jnp.bfloat16)

    rbuf[0, dp] = sbuf[0, dp]
    rbuf[1, dp] = sbuf[1, dp]

    def receive(part):
        a = part * CUT

        @pl.loop(0, NX)
        def _(ox):
            group = (x + NX - ox) % NX
            start = ox * rows_x

            @pl.loop(0, GROUP)
            def _(o):
                slot = ox * GROUP + o

                @pl.when(slot > 0)
                def _():
                    copy_rows(part, slot, peer(ox, o), peer_from(ox, o)).wait_recv()

            @pl.loop(0, GROUP // 2)
            def _(m):
                first = group * GROUP + 2 * m
                blocks = []
                for e in range(2):
                    got = rbuf[part, first + e].astype(F32)
                    blocks.append(jnp.concatenate([got[:CAP], got[CAP:]], axis=1))
                at = pl.multiple_of(first * CAP, 2 * CAP)
                gap = jnp.concatenate(blocks, axis=0) - part_ref[pl.ds(at, 2 * CAP), a:a + CUT].astype(F32)
                to = pl.multiple_of(start + m * 2 * CAP, 2 * CAP)
                diff_ref[pl.ds(to, 2 * CAP), a:a + CUT] = gap.astype(jnp.bfloat16)

            here = pl.ds(pl.multiple_of(start, rows_x), rows_x)
            for i in range(0, a + CUT, tile):
                b = max(i, a)
                gram_ref[i:i + tile, b:a + CUT] = gram_ref[i:i + tile, b:a + CUT] + pair_scale * lax.dot_general(
                    diff_ref[here, i:i + tile], diff_ref[here, b:a + CUT], contract_rows, preferred_element_type=F32)

    def metric(first_block, last_block):
        row = lax.broadcasted_iota(jnp.int32, (NB, NB), 0)
        col = lax.broadcasted_iota(jnp.int32, (NB, NB), 1)
        for i in range(last_block):
            a, b, e = i * NB, max(i, first_block) * NB, last_block * NB
            outer = lax.dot_general(mean_ref[:, a:a + NB], mean_ref[:, b:e], contract_rows,
                                    precision=HI, preferred_element_type=F32)
            c_ref[a:a + NB, b:e] = c_ref[a:a + NB, b:e] - shrink_weight * outer
            if i >= first_block:
                c_ref[a:a + NB, a:a + NB] = c_ref[a:a + NB, a:a + NB] + jnp.where(row == col, ridge_term, 0.0)

    receive(0)
    for r, c, at in segments(LEFT, DATA_LEFT, UNIT_LEFT):
        left.p[at:at + 8, :] = gram_ref[r:r + 8, c:c + NB]
    left.to_sibling()
    c_ref[...] = jnp.zeros((N, N), F32)
    mean_ref[...] = jnp.zeros((8, N), F32)
    left.to_plane()
    left.to_line()
    left.finish()
    means = left.out[DATA_LEFT:UNIT_LEFT, :] * (1.0 / rows_all)
    for i in range(BLOCKS):
        mean_ref[0:1, i * NB:(i + 1) * NB] = means[i:i + 1, :]
    for r, c, at in segments(LEFT, DATA_LEFT, UNIT_LEFT):
        c_ref[r:r + 8, c:c + NB] = left.out[at:at + 8, :]
    metric(0, BLOCKS // 2)

    receive(1)
    for r, c, at in segments(RIGHT, UNIT_RIGHT, UNIT_RIGHT):
        right.p[at:at + 8, :] = gram_ref[r:r + 8, c:c + NB]
    right.to_sibling()

    cut_block = BLOCKS // 2
    row = lax.broadcasted_iota(jnp.int32, (NB, NB), 0)
    col = lax.broadcasted_iota(jnp.int32, (NB, NB), 1)

    def step(k, _):
        @pl.when(k == 1)
        def _():
            right.to_plane()

        @pl.when(k == 3)
        def _():
            right.to_line()

        @pl.when(k == cut_block)
        def _():
            right.finish()
            for r, c, at in segments(RIGHT, UNIT_RIGHT, UNIT_RIGHT):
                c_ref[r:r + 8, c:c + NB] = right.out[at:at + 8, :]
            metric(cut_block, BLOCKS)
            r = lax.broadcasted_iota(jnp.int32, (CUT, CUT), 0)
            c = lax.broadcasted_iota(jnp.int32, (CUT, CUT), 1)
            gram_ref[0:CUT, 0:CUT] = jnp.where(r >= c, c_ref[0:CUT, 0:CUT], 0.0)
            upper = jnp.dot(gram_ref[0:CUT, 0:CUT], c_ref[0:CUT, CUT:], precision=HI, preferred_element_type=F32)
            c_ref[0:CUT, CUT:] = upper
            c_ref[CUT:, 0:CUT] = -lax.dot_general(c_ref[0:CUT, CUT:], gram_ref[0:CUT, 0:CUT], contract_rows,
                                                  precision=HI, preferred_element_type=F32)
            c_ref[CUT:, CUT:] = c_ref[CUT:, CUT:] - lax.dot_general(
                c_ref[0:CUT, CUT:], c_ref[0:CUT, CUT:], contract_rows, precision=HI, preferred_element_type=F32)

        off = pl.multiple_of(k * NB, NB)
        diag = c_ref.at[pl.ds(off, NB), pl.ds(off, NB)]
        rows = factor_block([diag[8 * q:8 * q + 8, :] for q in range(NB // 8)])
        for q in range(NB // 8):
            t_ref[8 * q:8 * q + 8, :] = rows[q]
        t = jnp.where(row >= col, t_ref[...], 0.0)

        @pl.when(k < cut_block)
        def _():
            c_ref[pl.ds(off, NB), 0:CUT] = jnp.dot(
                t, c_ref[pl.ds(off, NB), 0:CUT], precision=HI, preferred_element_type=F32)

        @pl.when(k >= cut_block)
        def _():
            c_ref[pl.ds(off, NB), :] = jnp.dot(
                t, c_ref[pl.ds(off, NB), :], precision=HI, preferred_element_type=F32)

        c_ref[pl.ds(off, NB), pl.ds(off, NB)] = t

        for now in range(BLOCKS - 1):
            if now == cut_block - 1:
                continue

            @pl.when(k == now)
            def _(now=now):
                at, nxt = now * NB, (now + 1) * NB
                end = CUT if now < cut_block else N
                u = c_ref[at:nxt, nxt:end]
                prod = lax.dot_general(u, c_ref[at:nxt, 0:nxt], contract_rows, precision=HI,
                                       preferred_element_type=F32)
                if now:
                    c_ref[nxt:end, 0:at] = c_ref[nxt:end, 0:at] - prod[:, 0:at]
                c_ref[nxt:end, at:nxt] = -prod[:, at:nxt]
                for r in range(nxt, end, 2 * NB):
                    h = min(2 * NB, end - r)
                    prod = lax.dot_general(u[:, r - nxt:r - nxt + h], c_ref[at:nxt, r:end], contract_rows,
                                           precision=HI, preferred_element_type=F32)
                    c_ref[r:r + h, r:end] = c_ref[r:r + h, r:end] - prod
        return 0

    lax.fori_loop(0, BLOCKS, step, 0)
    for i in range(BLOCKS):
        r = lax.broadcasted_iota(jnp.int32, (NB, N), 0) + i * NB
        c = lax.broadcasted_iota(jnp.int32, (NB, N), 1)
        a = i * NB
        out_ref[a:a + NB, :] = jnp.where(r >= c, c_ref[a:a + NB, :], 0.0).astype(jnp.bfloat16)

    @pl.loop(1, PEERS)
    def _(k):
        copy_rows(0, k, peer(k // GROUP, k % GROUP), dp).wait_send()
        copy_rows(1, k, peer(k // GROUP, k % GROUP), dp).wait_send()
        copy_index(k, peer(k // GROUP, k % GROUP), dp).wait_send()


def inverse_factor(pair_scale, row_scale, rows_all, anchor, wanted, descriptors):
    dma = pltpu.SemaphoreType.DMA

    def sum_scratch(unit, piece):
        half = PLANE * unit
        return [
            pltpu.VMEM((NC * half, NB), F32),
            pltpu.VMEM((NC * half, NB), F32),
            pltpu.VMEM((half, NB), F32),
            pltpu.VMEM((half, NB), F32),
            pltpu.VMEM((PLANE, unit, NB), F32),
            pltpu.VMEM((NZ * piece, NB), F32),
            pltpu.VMEM((NZ, piece, NB), F32),
            pltpu.VMEM((NZ * piece, NB), F32),
            dma((8, PLANE)),
            dma((4, NZ)),
        ]

    return pl.pallas_call(
        functools.partial(factor_kernel, pair_scale, row_scale, rows_all),
        out_shape=[jax.ShapeDtypeStruct((N, N), jnp.bfloat16), jax.ShapeDtypeStruct((8, N), F32)],
        in_specs=[pl.BlockSpec(memory_space=pltpu.VMEM)] * 3,
        out_specs=[pl.BlockSpec(memory_space=pltpu.VMEM)] * 2,
        scratch_shapes=[
            pltpu.VMEM((2, PEERS, 2 * CAP, CUT // 2), jnp.bfloat16),
            pltpu.VMEM((2, PEERS, 2 * CAP, CUT // 2), jnp.bfloat16),
            pltpu.VMEM((PEERS, 1, NB), F32),
            pltpu.VMEM((PEERS * CAP, NB), F32),
            pltpu.VMEM((PEERS * CAP, N), jnp.bfloat16),
            pltpu.VMEM((PEERS * CAP, N), jnp.bfloat16),
            pltpu.VMEM((N, N), F32),
            pltpu.VMEM((N, N), F32),
            pltpu.VMEM((NB, NB), F32),
            dma((2, PEERS)), dma((2, PEERS)), dma((PEERS,)), dma((PEERS,)),
        ] + sum_scratch(UNIT_LEFT, PIECE_LEFT) + sum_scratch(UNIT_RIGHT, PIECE_RIGHT),
        compiler_params=pltpu.CompilerParams(
            collective_id=1, has_side_effects=True, vmem_limit_bytes=56 << 20
        ),
    )(anchor, wanted, descriptors)


def whiten_kernel(db_ref, mean_ref, inv_ref, out_ref):
    centered = (db_ref[...].astype(F32) - mean_ref[0:1, :]).astype(jnp.bfloat16)
    projected = lax.dot_general(
        centered, inv_ref[...], (((1,), (1,)), ((), ())), preferred_element_type=F32
    )
    energy = jnp.mean(projected * projected, axis=1, keepdims=True)
    out_ref[...] = (projected * lax.rsqrt(energy + norm_epsilon)).astype(jnp.bfloat16)


def whiten(database, col_mean, inverse):
    rows, width = database.shape
    tile = 256
    return pl.pallas_call(
        whiten_kernel,
        grid=(rows // tile,),
        out_shape=jax.ShapeDtypeStruct((rows, width), jnp.bfloat16),
        in_specs=[
            pl.BlockSpec((tile, width), lambda i: (i, 0)),
            pl.BlockSpec((8, width), lambda i: (0, 0)),
            pl.BlockSpec((width, width), lambda i: (0, 0)),
        ],
        out_specs=pl.BlockSpec((tile, width), lambda i: (i, 0)),
        compiler_params=pltpu.CompilerParams(vmem_limit_bytes=40 << 20),
    )(database, col_mean, inverse)


def shards(descriptors, database, anchor_row, partner_row, block_counts):
    local_rows = descriptors.shape[0]
    peer_count = partner_row.shape[1]
    slot_count = partner_row.shape[2]
    devices = lax.axis_size("dp") * lax.axis_size("mp")
    pairs_all = PAIRS_DEV * devices
    rows_all = local_rows * devices
    slot_iota = lax.broadcasted_iota(jnp.int32, (peer_count, slot_count), 1)
    live_slots = slot_iota < block_counts[0][:, None]
    wanted = jnp.where(live_slots, partner_row[0], -1).astype(F32)
    wanted = jnp.pad(wanted, ((0, 0), (0, NB - slot_count)))[:, None, :]
    anchor = jnp.where(live_slots, anchor_row[0], -1).astype(F32).reshape(-1, 1)
    inverse, col_mean = inverse_factor(
        1.0 / pairs_all,
        shrink_weight / rows_all,
        rows_all,
        jnp.broadcast_to(anchor, (peer_count * slot_count, NB)),
        wanted,
        descriptors,
    )
    return whiten(database, col_mean, inverse)


def solution(mesh):
    placed = (
        P(("dp", "mp"), None),
        P(("dp", "mp"), None),
        P(("dp", "mp"), None, None),
        P(("dp", "mp"), None, None),
        P(("dp", "mp"), None),
    )
    return jax.shard_map(
        shards, mesh=mesh, in_specs=placed, out_specs=P(("dp", "mp"), None), check_vma=False
    )
```

```python
import functools

import jax
import jax.numpy as jnp
from jax import lax
from jax.experimental import pallas as pl
from jax.experimental.pallas import tpu as pltpu
from jax.sharding import PartitionSpec as P

PAIRS_DEV = 1024


shrink_weight = 0.5
ridge_term = 0.05
norm_epsilon = 1e-06
contract_rows = (((0,), (0,)), ((), ()))

N = 1024
NB = 128
F32 = jnp.float32
HI = lax.Precision.HIGHEST
MESH = pl.DeviceIdType.MESH

def lane_bcast(x, c):
    return jnp.take_along_axis(x, jnp.full(x.shape, c, jnp.int32), axis=1, mode="promise_in_bounds")


def row_bcast(x, i):
    return jnp.broadcast_to(x[i:i + 1, :], x.shape)


def factor_block(rows):
    lane = lax.broadcasted_iota(jnp.int32, (8, NB), 1)
    sub = lax.broadcasted_iota(jnp.int32, (8, NB), 0)
    count = len(rows)
    for q in range(count):
        base = 8 * q
        inside = (lane >= base) & (lane < base + 8)
        own = [row_bcast(rows[q], i) for i in range(8)]
        d = {}
        for j in range(8):
            for i in range(j, 8):
                d[i, j] = lane_bcast(own[i], base + j)
        w = [jnp.where(inside, jnp.where(lane == base + i, 1.0, 0.0), own[i]) for i in range(8)]
        ahead = q + 1 < count
        v = [lane_bcast(rows[q + 1], base + j) for j in range(8)] if ahead else None
        inv, scale, low = [], [], {}
        for j in range(8):
            s = lax.rsqrt(d[j, j])
            r = s * s
            inv.append(r)
            scale.append(s)
            for i in range(j + 1, 8):
                low[i, j] = d[i, j] * r
            for i in range(j + 1, 8):
                for k in range(j + 1, i + 1):
                    d[i, k] = d[i, k] - low[i, j] * d[k, j]
            for i in range(j + 1, 8):
                w[i] = w[i] - low[i, j] * w[j]
                if ahead:
                    v[i] = v[i] - low[i, j] * v[j]
        if ahead:
            following = jnp.where(inside, 0.0, rows[q + 1])
            for j in range(8):
                following = following - v[j] * (inv[j] * w[j])
        g = [None] * 8
        for i in range(7, -1, -1):
            acc = inv[i] * w[i]
            for j in range(i + 1, 8):
                acc = acc - low[j, i] * g[j]
            g[i] = acc
        out = scale[0] * w[0]
        for i in range(1, 8):
            out = jnp.where(sub == i, scale[i] * w[i], out)
        rows[q] = out
        for t in range(q + 2, count):
            acc = jnp.where(inside, 0.0, rows[t])
            for j in range(8):
                acc = acc - lane_bcast(rows[t], base + j) * g[j]
            rows[t] = acc
        if ahead:
            rows[q + 1] = following
    return rows


NX, NY, NZ, NC = 4, 4, 8, 2
PLANE = NX * NY
BLOCKS = N // NB
CAP = 24
GROUP = NZ * NC
PEERS = NX * GROUP
CUT = N // 2
LEFT = [(i, j) for j in range(BLOCKS // 2) for i in range(j + 1)]
RIGHT = [(i, j) for j in range(BLOCKS // 2, BLOCKS) for i in range(j + 1)]
DATA_LEFT = len(LEFT) * NB // (NC * PLANE)
UNIT_LEFT = DATA_LEFT + 8
UNIT_RIGHT = len(RIGHT) * NB // (NC * PLANE)
PIECE_LEFT, PIECE_RIGHT = 8, 16


def segments(blocks, data, unit):
    found = []
    for b, (i, j) in enumerate(blocks):
        for s in range(0, NB, 8):
            flat = b * NB + s
            found.append((i * NB + s, j * NB, flat // data * unit + flat % data))
    return found


def one_hot_rows(index, count):
    lane = lax.broadcasted_iota(jnp.int32, (count, NB), 1).astype(F32)
    parts = [jnp.where(index == lane + float(NB * c), 1.0, 0.0).astype(jnp.bfloat16) for c in range(N // NB)]
    return jnp.concatenate(parts, axis=1)


def rem(a, b):
    return a % b if isinstance(a, int) else lax.rem(a, b)


def div(a, b):
    return a // b if isinstance(a, int) else lax.div(a, b)


def rows_at(base, count):
    return pl.ds(pl.multiple_of(base, 8), count)


class Sum:
    def __init__(self, unit, piece, p_ref, out_ref, half, r0, r1, zb, r2, gz, near, far):
        self.unit, self.piece, self.half_rows = unit, piece, PLANE * unit
        self.p, self.out, self.half, self.r0, self.r1 = p_ref, out_ref, half, r0, r1
        self.zb, self.r2, self.gz, self.near, self.far = zb, r2, gz, near, far
        dp, self.y = lax.axis_index("dp"), lax.axis_index("mp")
        self.core, self.z, self.x = rem(dp, NC), rem(div(dp, NC), NZ), div(dp, NC * NZ)
        self.sibling = (dp + 1 - 2 * self.core, self.y)
        self.mine = self.x * NY + self.y

    def plane(self, o):
        return rem(self.x + div(o, NY), NX), rem(self.y + rem(o, NY), NY)

    def plane_from(self, o):
        return rem(self.x + NX - div(o, NY), NX), rem(self.y + NY - rem(o, NY), NY)

    def plane_id(self, o):
        tx, ty = self.plane(o)
        return ((tx * NZ + self.z) * NC + self.core, ty)

    def line_id(self, o):
        return ((self.x * NZ + rem(self.z + o, NZ)) * NC + self.core, self.y)

    def near_copy(self, pair, o, src, dst, target):
        return pltpu.make_async_remote_copy(
            src_ref=src, dst_ref=dst, send_sem=self.near.at[2 * pair, 0], recv_sem=self.near.at[2 * pair + 1, o],
            device_id=target, device_id_type=MESH)

    def far_copy(self, pair, src, dst, target):
        return pltpu.make_async_remote_copy(
            src_ref=src, dst_ref=dst, send_sem=self.far.at[2 * pair], recv_sem=self.far.at[2 * pair + 1],
            device_id=target, device_id_type=MESH)

    def unit_at(self, o):
        tx, ty = self.plane(o)
        return (tx * NY + ty) * self.unit

    def copy0(self, o):
        at = self.unit_at(o)
        src = self.p.at[rows_at((1 - self.core) * self.half_rows + at, self.unit)]
        return self.near_copy(0, o, src, self.r0.at[rows_at(at, self.unit)], self.sibling)

    def copy1(self, o):
        return self.near_copy(1, 0, self.half.at[rows_at(self.unit_at(o), self.unit)], self.r1.at[o], self.plane_id(o))

    def copy2(self, o):
        src = self.zb.at[rows_at((rem(self.z + o, NZ)) * self.piece, self.piece)]
        return self.far_copy(0, src, self.r2.at[o], self.line_id(o))

    def copy3(self, o, owner):
        part = self.gz.at[rows_at(owner * self.piece, self.piece)]
        return self.far_copy(1, part, part, self.line_id(o))

    def copy4(self, o, owner):
        dst = self.out.at[rows_at(self.core * self.half_rows + owner * self.unit, self.unit)]
        return self.near_copy(2, o, self.gz.at[pl.ds(0, self.unit)], dst, self.plane_id(o))

    def copy5(self, o, which):
        tx, ty = self.plane_from(o)
        part = self.out.at[rows_at(which * self.half_rows + (tx * NY + ty) * self.unit, self.unit)]
        return self.near_copy(3, 0, part, part, self.sibling)

    def to_sibling(self):
        @pl.loop(0, PLANE)
        def _(i):
            self.copy0((i + 1) % PLANE).start()

        pad = self.zb.shape[0] - self.unit
        self.zb[self.unit:, :] = jnp.zeros((pad, NB), F32)

    def to_plane(self):
        @pl.loop(1, PLANE)
        def _(o):
            self.copy0(o).wait_recv()
            at = self.unit_at(o)
            own = self.p[rows_at(self.core * self.half_rows + at, self.unit), :]
            self.half[rows_at(at, self.unit), :] = own + self.r0[rows_at(at, self.unit), :]
            self.copy1(o).start()

        self.copy0(0).wait_recv()
        at = self.mine * self.unit
        own = self.p[rows_at(self.core * self.half_rows + at, self.unit), :]
        self.zb[0:self.unit, :] = own + self.r0[rows_at(at, self.unit), :]

    def to_line(self):
        got = self.r1.at[pl.ds(1, PLANE - 1)]
        self.near_copy(1, 0, got, got, self.sibling).wait_recv()
        total = self.zb[0:self.unit, :]
        for o in range(1, PLANE):
            total = total + self.r1[o]
        self.zb[0:self.unit, :] = total

        @pl.loop(1, NZ)
        def _(o):
            self.copy2(o).start()

        own = rows_at(self.z * self.piece, self.piece)
        got = self.r2.at[pl.ds(1, NZ - 1)]
        self.far_copy(0, got, got, self.sibling).wait_recv()
        total = self.zb[own, :]
        for o in range(1, NZ):
            total = total + self.r2[o]
        self.gz[own, :] = total

        @pl.loop(1, NZ)
        def _(o):
            self.copy3(o, self.z).start()

        got = self.gz.at[pl.ds(0, (NZ - 1) * self.piece)]
        self.far_copy(1, got, got, self.sibling).wait_recv()

        @pl.loop(1, PLANE)
        def _(o):
            self.copy4(o, self.mine).start()

        self.out[rows_at(self.core * self.half_rows + self.mine * self.unit, self.unit), :] = self.gz[0:self.unit, :]
        self.copy5(0, self.core).start()

    def finish(self):
        @pl.loop(1, PLANE)
        def _(o):
            tx, ty = self.plane_from(o)
            self.copy4(o, tx * NY + ty).wait_recv()
            self.copy5(o, self.core).start()

        got = self.out.at[pl.ds(0, self.half_rows)]
        self.near_copy(3, 0, got, got, self.sibling).wait_recv()

    def drain(self):
        whole = self.p.at[pl.ds(0, self.half_rows)]
        others = self.p.at[pl.ds(0, self.half_rows - self.unit)]
        line = self.zb.at[pl.ds(0, (NZ - 1) * self.piece)]
        self.near_copy(0, 0, whole, whole, self.sibling).wait_send()
        self.near_copy(1, 0, others, others, self.sibling).wait_send()
        self.far_copy(0, line, line, self.sibling).wait_send()
        self.far_copy(1, line, line, self.sibling).wait_send()
        self.near_copy(2, 0, others, others, self.sibling).wait_send()
        self.near_copy(3, 0, whole, whole, self.sibling).wait_send()


def factor_kernel(pair_scale, row_scale, rows_all, anchor_ref, wanted_ref, desc_ref, out_ref, mean_ref,
                  sbuf, rbuf, windex, wcol, part_ref, diff_ref, gram_ref, c_ref, t_ref, s0, q0, s1, q1,
                  *sums):
    dp, y = lax.axis_index("dp"), lax.axis_index("mp")
    core, z, x = rem(dp, NC), rem(div(dp, NC), NZ), div(dp, NC * NZ)
    left = Sum(UNIT_LEFT, PIECE_LEFT, *sums[:10])
    right = Sum(UNIT_RIGHT, PIECE_RIGHT, *sums[10:])

    def peer(ox, o):
        return rem(x + ox, NX) * GROUP + rem(z + div(o, NC), NZ) * NC + rem(core + rem(o, NC), NC)

    def copy_rows(part, ox, target):
        return pltpu.make_async_remote_copy(
            src_ref=sbuf.at[part, target], dst_ref=rbuf.at[part, dp], send_sem=s0.at[part],
            recv_sem=q0.at[part, ox], device_id=(target, y), device_id_type=MESH)

    def rows_of(part, ox, count):
        return pltpu.make_async_remote_copy(
            src_ref=sbuf.at[part, pl.ds(0, count)], dst_ref=rbuf.at[part, pl.ds(0, count)], send_sem=s0.at[part],
            recv_sem=q0.at[part, ox], device_id=left.sibling, device_id_type=MESH)

    def copy_index(target):
        return pltpu.make_async_remote_copy(
            src_ref=wanted_ref.at[target], dst_ref=windex.at[dp], send_sem=s1.at[0], recv_sem=q1.at[0],
            device_id=(target, y), device_id_type=MESH)

    indices = pltpu.make_async_remote_copy(
        src_ref=wanted_ref.at[pl.ds(0, PEERS - 1)], dst_ref=windex.at[pl.ds(0, PEERS - 1)], send_sem=s1.at[0],
        recv_sem=q1.at[0], device_id=left.sibling, device_id_type=MESH)

    barrier = pltpu.get_barrier_semaphore()

    @pl.loop(1, PEERS)
    def _(k):
        pl.semaphore_signal(barrier, inc=1, device_id=(peer(div(k, GROUP), rem(k, GROUP)), y), device_id_type=MESH)

    @pl.loop(1, PLANE)
    def _(o):
        @pl.when(rem(o, NY) != 0)
        def _():
            pl.semaphore_signal(barrier, inc=1, device_id=left.plane_id(o), device_id_type=MESH)

    rows_x = GROUP * CAP

    def gather(ox):
        group = rem(x + ox, NX)
        base = group * rows_x
        for h in range(2):
            count = rows_x // 2
            index = anchor_ref[pl.ds(pl.multiple_of(base + h * count, count), count), :]
            found = jnp.dot(one_hot_rows(index, count), desc_ref[...], preferred_element_type=F32)
            for p in range(GROUP // 2):
                block = found[p * CAP:(p + 1) * CAP, :]
                for part in range(2):
                    a = part * CUT
                    halves = jnp.concatenate([block[:, a:a + CUT // 2], block[:, a + CUT // 2:a + CUT]], axis=0)
                    sbuf[part, group * GROUP + h * (GROUP // 2) + p] = halves.astype(jnp.bfloat16)

    gather(0)
    pl.semaphore_wait(barrier, PEERS - 1 + PLANE - NX)

    @pl.loop(0, NX)
    def _(ox):
        @pl.loop(0, GROUP)
        def _(o):
            @pl.when(ox * GROUP + o > 0)
            def _():
                copy_rows(0, ox, peer(ox, o)).start()

        @pl.when(ox == 0)
        def _():
            @pl.loop(1, PEERS)
            def _(k):
                copy_index(peer(div(k, GROUP), rem(k, GROUP))).start()

        @pl.when(ox < NX - 1)
        def _():
            gather(ox + 1)

    @pl.loop(1, PEERS)
    def _(k):
        copy_rows(1, div(k, GROUP), peer(div(k, GROUP), rem(k, GROUP))).start()

    tile = 256
    for i in range(0, N, tile):
        gram_ref[i:i + tile, i:] = row_scale * lax.dot_general(
            desc_ref[:, i:i + tile], desc_ref[:, i:], contract_rows, preferred_element_type=F32)
    ones = jnp.ones((8, desc_ref.shape[0]), jnp.bfloat16)
    sums_row = jnp.dot(ones, desc_ref[...], preferred_element_type=F32)
    sub = lax.broadcasted_iota(jnp.int32, (8, NB), 0)
    packed = sums_row[:, 0:NB]
    for i in range(1, BLOCKS):
        packed = jnp.where(sub == i, sums_row[:, i * NB:(i + 1) * NB], packed)
    for u in range(NC * PLANE):
        left.p[u * UNIT_LEFT + DATA_LEFT:(u + 1) * UNIT_LEFT, :] = packed

    windex[dp] = wanted_ref[dp]

    indices.wait_recv()
    turned = windex[...].reshape(PEERS, NB)
    turned = jnp.concatenate([turned, jnp.zeros((NB - PEERS, NB), F32)], axis=0).T
    for p in range(PEERS):
        wcol[p * CAP:(p + 1) * CAP, :] = jnp.broadcast_to(turned[0:CAP, p:p + 1], (CAP, NB))

    count = 192

    @pl.loop(0, PEERS * CAP // count)
    def _(g):
        at = pl.ds(pl.multiple_of(g * count, count), count)
        found = jnp.dot(one_hot_rows(wcol[at, :], count), desc_ref[...], preferred_element_type=F32)
        part_ref[at, :] = found.astype(jnp.bfloat16)

    rbuf[0, dp] = sbuf[0, dp]
    rbuf[1, dp] = sbuf[1, dp]

    def receive(part):
        a = part * CUT

        @pl.loop(0, NX)
        def _(ox):
            group = rem(x + NX - ox, NX)
            start = ox * rows_x

            @pl.when(ox == 0)
            def _():
                rows_of(part, ox, GROUP - 1).wait_recv()

            @pl.when(ox > 0)
            def _():
                rows_of(part, ox, GROUP).wait_recv()

            @pl.loop(0, GROUP // 2)
            def _(m):
                first = group * GROUP + 2 * m
                blocks = []
                for e in range(2):
                    got = rbuf[part, first + e].astype(F32)
                    blocks.append(jnp.concatenate([got[:CAP], got[CAP:]], axis=1))
                at = pl.multiple_of(first * CAP, 2 * CAP)
                gap = jnp.concatenate(blocks, axis=0) - part_ref[pl.ds(at, 2 * CAP), a:a + CUT].astype(F32)
                to = pl.multiple_of(start + m * 2 * CAP, 2 * CAP)
                diff_ref[pl.ds(to, 2 * CAP), a:a + CUT] = gap.astype(jnp.bfloat16)

            here = pl.ds(pl.multiple_of(start, rows_x), rows_x)
            for i in range(0, a + CUT, tile):
                b = max(i, a)
                gram_ref[i:i + tile, b:a + CUT] = gram_ref[i:i + tile, b:a + CUT] + pair_scale * lax.dot_general(
                    diff_ref[here, i:i + tile], diff_ref[here, b:a + CUT], contract_rows, preferred_element_type=F32)

    def metric(first_block, last_block):
        row = lax.broadcasted_iota(jnp.int32, (NB, NB), 0)
        col = lax.broadcasted_iota(jnp.int32, (NB, NB), 1)
        for i in range(last_block):
            a, b, e = i * NB, max(i, first_block) * NB, last_block * NB
            outer = lax.dot_general(mean_ref[:, a:a + NB], mean_ref[:, b:e], contract_rows,
                                    precision=HI, preferred_element_type=F32)
            c_ref[a:a + NB, b:e] = c_ref[a:a + NB, b:e] - shrink_weight * outer
            if i >= first_block:
                c_ref[a:a + NB, a:a + NB] = c_ref[a:a + NB, a:a + NB] + jnp.where(row == col, ridge_term, 0.0)

    receive(0)
    for r, c, at in segments(LEFT, DATA_LEFT, UNIT_LEFT):
        left.p[at:at + 8, :] = gram_ref[r:r + 8, c:c + NB]
    left.to_sibling()
    c_ref[...] = jnp.zeros((N, N), F32)
    mean_ref[...] = jnp.zeros((8, N), F32)
    left.to_plane()
    left.to_line()
    left.finish()
    means = left.out[DATA_LEFT:UNIT_LEFT, :] * (1.0 / rows_all)
    for i in range(BLOCKS):
        mean_ref[0:1, i * NB:(i + 1) * NB] = means[i:i + 1, :]
    for r, c, at in segments(LEFT, DATA_LEFT, UNIT_LEFT):
        c_ref[r:r + 8, c:c + NB] = left.out[at:at + 8, :]
    metric(0, BLOCKS // 2)

    receive(1)
    for r, c, at in segments(RIGHT, UNIT_RIGHT, UNIT_RIGHT):
        right.p[at:at + 8, :] = gram_ref[r:r + 8, c:c + NB]
    right.to_sibling()

    cut_block = BLOCKS // 2
    row = lax.broadcasted_iota(jnp.int32, (NB, NB), 0)
    col = lax.broadcasted_iota(jnp.int32, (NB, NB), 1)

    def step(k, _):
        @pl.when(k == 1)
        def _():
            right.to_plane()
            left.drain()
            rows_of(0, 0, PEERS - 1).wait_send()
            rows_of(1, 0, PEERS - 1).wait_send()
            indices.wait_send()

        @pl.when(k == 3)
        def _():
            right.to_line()

        @pl.when(k == cut_block)
        def _():
            right.finish()
            for r, c, at in segments(RIGHT, UNIT_RIGHT, UNIT_RIGHT):
                c_ref[r:r + 8, c:c + NB] = right.out[at:at + 8, :]
            metric(cut_block, BLOCKS)
            r = lax.broadcasted_iota(jnp.int32, (CUT, CUT), 0)
            c = lax.broadcasted_iota(jnp.int32, (CUT, CUT), 1)
            gram_ref[0:CUT, 0:CUT] = jnp.where(r >= c, c_ref[0:CUT, 0:CUT], 0.0)
            upper = jnp.dot(gram_ref[0:CUT, 0:CUT], c_ref[0:CUT, CUT:], precision=HI, preferred_element_type=F32)
            c_ref[0:CUT, CUT:] = upper
            c_ref[CUT:, 0:CUT] = -lax.dot_general(c_ref[0:CUT, CUT:], gram_ref[0:CUT, 0:CUT], contract_rows,
                                                  precision=HI, preferred_element_type=F32)
            c_ref[CUT:, CUT:] = c_ref[CUT:, CUT:] - lax.dot_general(
                c_ref[0:CUT, CUT:], c_ref[0:CUT, CUT:], contract_rows, precision=HI, preferred_element_type=F32)

        off = pl.multiple_of(k * NB, NB)
        diag = c_ref.at[pl.ds(off, NB), pl.ds(off, NB)]
        rows = factor_block([diag[8 * q:8 * q + 8, :] for q in range(NB // 8)])
        for q in range(NB // 8):
            t_ref[8 * q:8 * q + 8, :] = rows[q]
        t = jnp.where(row >= col, t_ref[...], 0.0)

        @pl.when(k < cut_block)
        def _():
            c_ref[pl.ds(off, NB), 0:CUT] = jnp.dot(
                t, c_ref[pl.ds(off, NB), 0:CUT], precision=HI, preferred_element_type=F32)

        @pl.when(k >= cut_block)
        def _():
            c_ref[pl.ds(off, NB), :] = jnp.dot(
                t, c_ref[pl.ds(off, NB), :], precision=HI, preferred_element_type=F32)

        c_ref[pl.ds(off, NB), pl.ds(off, NB)] = t

        for now in range(BLOCKS - 1):
            if now == cut_block - 1:
                continue

            @pl.when(k == now)
            def _(now=now):
                at, nxt = now * NB, (now + 1) * NB
                end = CUT if now < cut_block else N
                u = c_ref[at:nxt, nxt:end]
                prod = lax.dot_general(u, c_ref[at:nxt, 0:nxt], contract_rows, precision=HI,
                                       preferred_element_type=F32)
                if now:
                    c_ref[nxt:end, 0:at] = c_ref[nxt:end, 0:at] - prod[:, 0:at]
                c_ref[nxt:end, at:nxt] = -prod[:, at:nxt]
                for r in range(nxt, end, 2 * NB):
                    h = min(2 * NB, end - r)
                    prod = lax.dot_general(u[:, r - nxt:r - nxt + h], c_ref[at:nxt, r:end], contract_rows,
                                           precision=HI, preferred_element_type=F32)
                    c_ref[r:r + h, r:end] = c_ref[r:r + h, r:end] - prod
        return 0

    lax.fori_loop(0, BLOCKS, step, 0)
    for i in range(BLOCKS):
        r = lax.broadcasted_iota(jnp.int32, (NB, N), 0) + i * NB
        c = lax.broadcasted_iota(jnp.int32, (NB, N), 1)
        a = i * NB
        out_ref[a:a + NB, :] = jnp.where(r >= c, c_ref[a:a + NB, :], 0.0).astype(jnp.bfloat16)

    right.drain()


def inverse_factor(pair_scale, row_scale, rows_all, anchor, wanted, descriptors):
    dma = pltpu.SemaphoreType.DMA

    def sum_scratch(unit, piece):
        half = PLANE * unit
        return [
            pltpu.VMEM((NC * half, NB), F32),
            pltpu.VMEM((NC * half, NB), F32),
            pltpu.VMEM((half, NB), F32),
            pltpu.VMEM((half, NB), F32),
            pltpu.VMEM((PLANE, unit, NB), F32),
            pltpu.VMEM((NZ * piece, NB), F32),
            pltpu.VMEM((NZ, piece, NB), F32),
            pltpu.VMEM((NZ * piece, NB), F32),
            dma((8, PLANE)),
            dma((4,)),
        ]

    return pl.pallas_call(
        functools.partial(factor_kernel, pair_scale, row_scale, rows_all),
        out_shape=[jax.ShapeDtypeStruct((N, N), jnp.bfloat16), jax.ShapeDtypeStruct((8, N), F32)],
        in_specs=[pl.BlockSpec(memory_space=pltpu.VMEM)] * 3,
        out_specs=[pl.BlockSpec(memory_space=pltpu.VMEM)] * 2,
        scratch_shapes=[
            pltpu.VMEM((2, PEERS, 2 * CAP, CUT // 2), jnp.bfloat16),
            pltpu.VMEM((2, PEERS, 2 * CAP, CUT // 2), jnp.bfloat16),
            pltpu.VMEM((PEERS, 1, NB), F32),
            pltpu.VMEM((PEERS * CAP, NB), F32),
            pltpu.VMEM((PEERS * CAP, N), jnp.bfloat16),
            pltpu.VMEM((PEERS * CAP, N), jnp.bfloat16),
            pltpu.VMEM((N, N), F32),
            pltpu.VMEM((N, N), F32),
            pltpu.VMEM((NB, NB), F32),
            dma((2,)), dma((2, NX)), dma((1,)), dma((1,)),
        ] + sum_scratch(UNIT_LEFT, PIECE_LEFT) + sum_scratch(UNIT_RIGHT, PIECE_RIGHT),
        compiler_params=pltpu.CompilerParams(
            collective_id=1, has_side_effects=True, vmem_limit_bytes=56 << 20
        ),
    )(anchor, wanted, descriptors)


def whiten_kernel(db_ref, mean_ref, inv_ref, out_ref):
    centered = (db_ref[...].astype(F32) - mean_ref[0:1, :]).astype(jnp.bfloat16)
    projected = lax.dot_general(
        centered, inv_ref[...], (((1,), (1,)), ((), ())), preferred_element_type=F32
    )
    energy = jnp.mean(projected * projected, axis=1, keepdims=True)
    out_ref[...] = (projected * lax.rsqrt(energy + norm_epsilon)).astype(jnp.bfloat16)


def whiten(database, col_mean, inverse):
    rows, width = database.shape
    tile = 256
    return pl.pallas_call(
        whiten_kernel,
        grid=(rows // tile,),
        out_shape=jax.ShapeDtypeStruct((rows, width), jnp.bfloat16),
        in_specs=[
            pl.BlockSpec((tile, width), lambda i: (i, 0)),
            pl.BlockSpec(memory_space=pltpu.VMEM),
            pl.BlockSpec(memory_space=pltpu.VMEM),
        ],
        out_specs=pl.BlockSpec((tile, width), lambda i: (i, 0)),
        compiler_params=pltpu.CompilerParams(vmem_limit_bytes=40 << 20),
    )(database, col_mean, inverse)


def shards(descriptors, database, anchor_row, partner_row, block_counts):
    local_rows = descriptors.shape[0]
    peer_count = partner_row.shape[1]
    slot_count = partner_row.shape[2]
    devices = lax.axis_size("dp") * lax.axis_size("mp")
    pairs_all = PAIRS_DEV * devices
    rows_all = local_rows * devices
    slot_iota = lax.broadcasted_iota(jnp.int32, (peer_count, slot_count), 1)
    live_slots = slot_iota < block_counts[0][:, None]
    wanted = jnp.where(live_slots, partner_row[0], -1).astype(F32)
    wanted = jnp.pad(wanted, ((0, 0), (0, NB - slot_count)))[:, None, :]
    anchor = jnp.where(live_slots, anchor_row[0], -1).astype(F32).reshape(-1, 1)
    inverse, col_mean = inverse_factor(
        1.0 / pairs_all,
        shrink_weight / rows_all,
        rows_all,
        jnp.broadcast_to(anchor, (peer_count * slot_count, NB)),
        wanted,
        descriptors,
    )
    return whiten(database, col_mean, inverse)


def solution(mesh):
    placed = (
        P(("dp", "mp"), None),
        P(("dp", "mp"), None),
        P(("dp", "mp"), None, None),
        P(("dp", "mp"), None, None),
        P(("dp", "mp"), None),
    )
    return jax.shard_map(
        shards, mesh=mesh, in_specs=placed, out_specs=P(("dp", "mp"), None), check_vma=False
    )
```

```python
import functools

import jax
import jax.numpy as jnp
from jax import lax
from jax.experimental import pallas as pl
from jax.experimental.pallas import tpu as pltpu
from jax.sharding import PartitionSpec as P

PAIRS_DEV = 1024


shrink_weight = 0.5
ridge_term = 0.05
norm_epsilon = 1e-06
contract_rows = (((0,), (0,)), ((), ()))

N = 1024
NB = 128
F32 = jnp.float32
HI = lax.Precision.HIGHEST
MESH = pl.DeviceIdType.MESH

def lane_bcast(x, c):
    return jnp.take_along_axis(x, jnp.full(x.shape, c, jnp.int32), axis=1, mode="promise_in_bounds")


def row_bcast(x, i):
    return jnp.broadcast_to(x[i:i + 1, :], x.shape)


def factor_block(rows):
    lane = lax.broadcasted_iota(jnp.int32, (8, NB), 1)
    sub = lax.broadcasted_iota(jnp.int32, (8, NB), 0)
    count = len(rows)
    for q in range(count):
        base = 8 * q
        inside = (lane >= base) & (lane < base + 8)
        own = [row_bcast(rows[q], i) for i in range(8)]
        d = {}
        for j in range(8):
            for i in range(j, 8):
                d[i, j] = lane_bcast(own[i], base + j)
        w = [jnp.where(inside, jnp.where(lane == base + i, 1.0, 0.0), own[i]) for i in range(8)]
        ahead = q + 1 < count
        v = [lane_bcast(rows[q + 1], base + j) for j in range(8)] if ahead else None
        inv, scale, low = [], [], {}
        for j in range(8):
            s = lax.rsqrt(d[j, j])
            r = s * s
            inv.append(r)
            scale.append(s)
            for i in range(j + 1, 8):
                low[i, j] = d[i, j] * r
            for i in range(j + 1, 8):
                for k in range(j + 1, i + 1):
                    d[i, k] = d[i, k] - low[i, j] * d[k, j]
            for i in range(j + 1, 8):
                w[i] = w[i] - low[i, j] * w[j]
                if ahead:
                    v[i] = v[i] - low[i, j] * v[j]
        if ahead:
            following = jnp.where(inside, 0.0, rows[q + 1])
            for j in range(8):
                following = following - v[j] * (inv[j] * w[j])
        g = [None] * 8
        for i in range(7, -1, -1):
            acc = inv[i] * w[i]
            for j in range(i + 1, 8):
                acc = acc - low[j, i] * g[j]
            g[i] = acc
        out = scale[0] * w[0]
        for i in range(1, 8):
            out = jnp.where(sub == i, scale[i] * w[i], out)
        rows[q] = out
        for t in range(q + 2, count):
            acc = jnp.where(inside, 0.0, rows[t])
            for j in range(8):
                acc = acc - lane_bcast(rows[t], base + j) * g[j]
            rows[t] = acc
        if ahead:
            rows[q + 1] = following
    return rows


NX, NY, NZ, NC = 4, 4, 8, 2
PLANE = NX * NY
BLOCKS = N // NB
CAP = 24
GROUP = NZ * NC
PEERS = NX * GROUP
CUT = N // 2
LEFT = [(i, j) for j in range(BLOCKS // 2) for i in range(j + 1)]
RIGHT = [(i, j) for j in range(BLOCKS // 2, BLOCKS) for i in range(j + 1)]
DATA_LEFT = len(LEFT) * NB // (NC * PLANE)
UNIT_LEFT = DATA_LEFT + 8
UNIT_RIGHT = len(RIGHT) * NB // (NC * PLANE)
PIECE_LEFT, PIECE_RIGHT = 8, 16


def segments(blocks, data, unit):
    found = []
    for b, (i, j) in enumerate(blocks):
        for s in range(0, NB, 8):
            flat = b * NB + s
            found.append((i * NB + s, j * NB, flat // data * unit + flat % data))
    return found


def one_hot_rows(index, count):
    lane = lax.broadcasted_iota(jnp.int32, (count, NB), 1).astype(F32)
    parts = [jnp.where(index == lane + float(NB * c), 1.0, 0.0).astype(jnp.bfloat16) for c in range(N // NB)]
    return jnp.concatenate(parts, axis=1)


def rem(a, b):
    return a % b if isinstance(a, int) else lax.rem(a, b)


def div(a, b):
    return a // b if isinstance(a, int) else lax.div(a, b)


def rows_at(base, count):
    return pl.ds(pl.multiple_of(base, 8), count)


class Sum:
    def __init__(self, unit, piece, p_ref, out_ref, half, r0, r1, zb, r2, gz, near, far):
        self.unit, self.piece, self.half_rows = unit, piece, PLANE * unit
        self.p, self.out, self.half, self.r0, self.r1 = p_ref, out_ref, half, r0, r1
        self.zb, self.r2, self.gz, self.near, self.far = zb, r2, gz, near, far
        dp, self.y = lax.axis_index("dp"), lax.axis_index("mp")
        self.core, self.z, self.x = rem(dp, NC), rem(div(dp, NC), NZ), div(dp, NC * NZ)
        self.sibling = (dp + 1 - 2 * self.core, self.y)
        self.mine = self.x * NY + self.y

    def plane(self, o):
        return rem(self.x + div(o, NY), NX), rem(self.y + rem(o, NY), NY)

    def plane_from(self, o):
        return rem(self.x + NX - div(o, NY), NX), rem(self.y + NY - rem(o, NY), NY)

    def plane_id(self, o):
        tx, ty = self.plane(o)
        return ((tx * NZ + self.z) * NC + self.core, ty)

    def line_id(self, o):
        return ((self.x * NZ + rem(self.z + o, NZ)) * NC + self.core, self.y)

    def near_copy(self, pair, o, src, dst, target):
        return pltpu.make_async_remote_copy(
            src_ref=src, dst_ref=dst, send_sem=self.near.at[2 * pair, 0], recv_sem=self.near.at[2 * pair + 1, o],
            device_id=target, device_id_type=MESH)

    def far_copy(self, pair, src, dst, target):
        return pltpu.make_async_remote_copy(
            src_ref=src, dst_ref=dst, send_sem=self.far.at[2 * pair], recv_sem=self.far.at[2 * pair + 1],
            device_id=target, device_id_type=MESH)

    def unit_at(self, o):
        tx, ty = self.plane(o)
        return (tx * NY + ty) * self.unit

    def copy0(self, o):
        at = self.unit_at(o)
        src = self.p.at[rows_at((1 - self.core) * self.half_rows + at, self.unit)]
        return self.near_copy(0, o, src, self.r0.at[rows_at(at, self.unit)], self.sibling)

    def copy1(self, o):
        return self.near_copy(1, 0, self.half.at[rows_at(self.unit_at(o), self.unit)], self.r1.at[o], self.plane_id(o))

    def copy2(self, o):
        src = self.zb.at[rows_at((rem(self.z + o, NZ)) * self.piece, self.piece)]
        return self.far_copy(0, src, self.r2.at[o], self.line_id(o))

    def copy3(self, o, owner):
        part = self.gz.at[rows_at(owner * self.piece, self.piece)]
        return self.far_copy(1, part, part, self.line_id(o))

    def copy4(self, o, owner):
        dst = self.out.at[rows_at(self.core * self.half_rows + owner * self.unit, self.unit)]
        return self.near_copy(2, o, self.gz.at[pl.ds(0, self.unit)], dst, self.plane_id(o))

    def copy5(self, o, which):
        tx, ty = self.plane_from(o)
        part = self.out.at[rows_at(which * self.half_rows + (tx * NY + ty) * self.unit, self.unit)]
        return self.near_copy(3, 0, part, part, self.sibling)

    def to_sibling(self):
        @pl.loop(0, PLANE)
        def _(i):
            self.copy0((i + 1) % PLANE).start()

        pad = self.zb.shape[0] - self.unit
        self.zb[self.unit:, :] = jnp.zeros((pad, NB), F32)

    def to_plane(self):
        @pl.loop(1, PLANE)
        def _(o):
            self.copy0(o).wait_recv()
            at = self.unit_at(o)
            own = self.p[rows_at(self.core * self.half_rows + at, self.unit), :]
            self.half[rows_at(at, self.unit), :] = own + self.r0[rows_at(at, self.unit), :]
            self.copy1(o).start()

        self.copy0(0).wait_recv()
        at = self.mine * self.unit
        own = self.p[rows_at(self.core * self.half_rows + at, self.unit), :]
        self.zb[0:self.unit, :] = own + self.r0[rows_at(at, self.unit), :]

    def to_line(self):
        got = self.r1.at[pl.ds(1, PLANE - 1)]
        self.near_copy(1, 0, got, got, self.sibling).wait_recv()
        total = self.zb[0:self.unit, :]
        for o in range(1, PLANE):
            total = total + self.r1[o]
        self.zb[0:self.unit, :] = total

        @pl.loop(1, NZ)
        def _(o):
            self.copy2(o).start()

        own = rows_at(self.z * self.piece, self.piece)
        got = self.r2.at[pl.ds(1, NZ - 1)]
        self.far_copy(0, got, got, self.sibling).wait_recv()
        total = self.zb[own, :]
        for o in range(1, NZ):
            total = total + self.r2[o]
        self.gz[own, :] = total

        @pl.loop(1, NZ)
        def _(o):
            self.copy3(o, self.z).start()

        got = self.gz.at[pl.ds(0, (NZ - 1) * self.piece)]
        self.far_copy(1, got, got, self.sibling).wait_recv()

        @pl.loop(1, PLANE)
        def _(o):
            self.copy4(o, self.mine).start()

        self.out[rows_at(self.core * self.half_rows + self.mine * self.unit, self.unit), :] = self.gz[0:self.unit, :]
        self.copy5(0, self.core).start()

    def finish(self):
        @pl.loop(1, PLANE)
        def _(o):
            tx, ty = self.plane_from(o)
            self.copy4(o, tx * NY + ty).wait_recv()
            self.copy5(o, self.core).start()

        got = self.out.at[pl.ds(0, self.half_rows)]
        self.near_copy(3, 0, got, got, self.sibling).wait_recv()

    def drain(self):
        whole = self.p.at[pl.ds(0, self.half_rows)]
        others = self.p.at[pl.ds(0, self.half_rows - self.unit)]
        line = self.zb.at[pl.ds(0, (NZ - 1) * self.piece)]
        self.near_copy(0, 0, whole, whole, self.sibling).wait_send()
        self.near_copy(1, 0, others, others, self.sibling).wait_send()
        self.far_copy(0, line, line, self.sibling).wait_send()
        self.far_copy(1, line, line, self.sibling).wait_send()
        self.near_copy(2, 0, others, others, self.sibling).wait_send()
        self.near_copy(3, 0, whole, whole, self.sibling).wait_send()


def factor_kernel(pair_scale, row_scale, rows_all, anchor_ref, wanted_ref, desc_ref, out_ref, mean_ref,
                  sbuf, rbuf, windex, wcol, part_ref, diff_ref, gram_ref, c_ref, t_ref, s0, q0, s1, q1,
                  *sums):
    dp, y = lax.axis_index("dp"), lax.axis_index("mp")
    core, z, x = rem(dp, NC), rem(div(dp, NC), NZ), div(dp, NC * NZ)
    left = Sum(UNIT_LEFT, PIECE_LEFT, *sums[:10])
    right = Sum(UNIT_RIGHT, PIECE_RIGHT, *sums[10:])

    def peer(ox, o):
        return rem(x + ox, NX) * GROUP + rem(z + div(o, NC), NZ) * NC + rem(core + rem(o, NC), NC)

    def copy_rows(part, ox, target):
        return pltpu.make_async_remote_copy(
            src_ref=sbuf.at[part, target], dst_ref=rbuf.at[part, dp], send_sem=s0.at[part],
            recv_sem=q0.at[part, ox], device_id=(target, y), device_id_type=MESH)

    def rows_of(part, ox, count):
        return pltpu.make_async_remote_copy(
            src_ref=sbuf.at[part, pl.ds(0, count)], dst_ref=rbuf.at[part, pl.ds(0, count)], send_sem=s0.at[part],
            recv_sem=q0.at[part, ox], device_id=left.sibling, device_id_type=MESH)

    def copy_index(target):
        return pltpu.make_async_remote_copy(
            src_ref=wanted_ref.at[target], dst_ref=windex.at[dp], send_sem=s1.at[0], recv_sem=q1.at[0],
            device_id=(target, y), device_id_type=MESH)

    indices = pltpu.make_async_remote_copy(
        src_ref=wanted_ref.at[pl.ds(0, PEERS - 1)], dst_ref=windex.at[pl.ds(0, PEERS - 1)], send_sem=s1.at[0],
        recv_sem=q1.at[0], device_id=left.sibling, device_id_type=MESH)

    barrier = pltpu.get_barrier_semaphore()

    @pl.loop(1, PEERS)
    def _(k):
        pl.semaphore_signal(barrier, inc=1, device_id=(peer(div(k, GROUP), rem(k, GROUP)), y), device_id_type=MESH)

    @pl.loop(1, PLANE)
    def _(o):
        @pl.when(rem(o, NY) != 0)
        def _():
            pl.semaphore_signal(barrier, inc=1, device_id=left.plane_id(o), device_id_type=MESH)

    rows_x = GROUP * CAP

    def gather(ox):
        group = rem(x + ox, NX)
        base = group * rows_x
        for h in range(2):
            count = rows_x // 2
            index = wcol[pl.ds(pl.multiple_of(base + h * count, count), count), :]
            found = jnp.dot(one_hot_rows(index, count), desc_ref[...], preferred_element_type=F32)
            for p in range(GROUP // 2):
                block = found[p * CAP:(p + 1) * CAP, :]
                for part in range(2):
                    a = part * CUT
                    halves = jnp.concatenate([block[:, a:a + CUT // 2], block[:, a + CUT // 2:a + CUT]], axis=0)
                    sbuf[part, group * GROUP + h * (GROUP // 2) + p] = halves.astype(jnp.bfloat16)

    def turn(rows):
        turned = jnp.concatenate([rows.reshape(PEERS, NB), jnp.zeros((NB - PEERS, NB), F32)], axis=0).T
        for p in range(PEERS):
            wcol[p * CAP:(p + 1) * CAP, :] = jnp.broadcast_to(turned[0:CAP, p:p + 1], (CAP, NB))

    turn(anchor_ref[...])
    gather(0)
    pl.semaphore_wait(barrier, PEERS - 1 + PLANE - NX)

    @pl.loop(0, NX)
    def _(ox):
        @pl.loop(0, GROUP)
        def _(o):
            @pl.when(ox * GROUP + o > 0)
            def _():
                copy_rows(0, ox, peer(ox, o)).start()

        @pl.when(ox == 0)
        def _():
            @pl.loop(1, PEERS)
            def _(k):
                copy_index(peer(div(k, GROUP), rem(k, GROUP))).start()

        @pl.when(ox < NX - 1)
        def _():
            gather(ox + 1)

    def send_right(ox):
        @pl.loop(0 if ox else 1, GROUP)
        def _(o):
            copy_rows(1, ox, peer(ox, o)).start()

    tile = 256
    for i in range(0, N, tile):
        gram_ref[i:i + tile, i:] = row_scale * lax.dot_general(
            desc_ref[:, i:i + tile], desc_ref[:, i:], contract_rows, preferred_element_type=F32)
    ones = jnp.ones((8, desc_ref.shape[0]), jnp.bfloat16)
    sums_row = jnp.dot(ones, desc_ref[...], preferred_element_type=F32)
    sub = lax.broadcasted_iota(jnp.int32, (8, NB), 0)
    packed = sums_row[:, 0:NB]
    for i in range(1, BLOCKS):
        packed = jnp.where(sub == i, sums_row[:, i * NB:(i + 1) * NB], packed)
    for u in range(NC * PLANE):
        left.p[u * UNIT_LEFT + DATA_LEFT:(u + 1) * UNIT_LEFT, :] = packed

    windex[dp] = wanted_ref[dp]

    indices.wait_recv()
    turn(windex[...])

    count = 192

    @pl.loop(0, PEERS * CAP // count)
    def _(g):
        at = pl.ds(pl.multiple_of(g * count, count), count)
        found = jnp.dot(one_hot_rows(wcol[at, :], count), desc_ref[...], preferred_element_type=F32)
        part_ref[at, :] = found.astype(jnp.bfloat16)

    rbuf[0, dp] = sbuf[0, dp]
    rbuf[1, dp] = sbuf[1, dp]

    def receive(part):
        a = part * CUT

        @pl.loop(0, NX)
        def _(ox):
            group = rem(x + NX - ox, NX)
            start = ox * rows_x

            @pl.when(ox == 0)
            def _():
                rows_of(part, ox, GROUP - 1).wait_recv()

            @pl.when(ox > 0)
            def _():
                rows_of(part, ox, GROUP).wait_recv()

            if part == 0:
                @pl.when(ox == 2)
                def _():
                    send_right(0)

            @pl.loop(0, GROUP // 2)
            def _(m):
                first = group * GROUP + 2 * m
                blocks = []
                for e in range(2):
                    got = rbuf[part, first + e].astype(F32)
                    blocks.append(jnp.concatenate([got[:CAP], got[CAP:]], axis=1))
                at = pl.multiple_of(first * CAP, 2 * CAP)
                gap = jnp.concatenate(blocks, axis=0) - part_ref[pl.ds(at, 2 * CAP), a:a + CUT].astype(F32)
                to = pl.multiple_of(start + m * 2 * CAP, 2 * CAP)
                diff_ref[pl.ds(to, 2 * CAP), a:a + CUT] = gap.astype(jnp.bfloat16)

            here = pl.ds(pl.multiple_of(start, rows_x), rows_x)
            for i in range(0, a + CUT, tile):
                b = max(i, a)
                gram_ref[i:i + tile, b:a + CUT] = gram_ref[i:i + tile, b:a + CUT] + pair_scale * lax.dot_general(
                    diff_ref[here, i:i + tile], diff_ref[here, b:a + CUT], contract_rows, preferred_element_type=F32)

    def metric(first_block, last_block):
        row = lax.broadcasted_iota(jnp.int32, (NB, NB), 0)
        col = lax.broadcasted_iota(jnp.int32, (NB, NB), 1)
        for i in range(last_block):
            a, b, e = i * NB, max(i, first_block) * NB, last_block * NB
            outer = lax.dot_general(mean_ref[:, a:a + NB], mean_ref[:, b:e], contract_rows,
                                    precision=HI, preferred_element_type=F32)
            c_ref[a:a + NB, b:e] = c_ref[a:a + NB, b:e] - shrink_weight * outer
            if i >= first_block:
                c_ref[a:a + NB, a:a + NB] = c_ref[a:a + NB, a:a + NB] + jnp.where(row == col, ridge_term, 0.0)

    receive(0)
    for r, c, at in segments(LEFT, DATA_LEFT, UNIT_LEFT):
        left.p[at:at + 8, :] = gram_ref[r:r + 8, c:c + NB]
    left.to_sibling()
    send_right(1)
    c_ref[...] = jnp.zeros((N, N), F32)
    mean_ref[...] = jnp.zeros((8, N), F32)
    left.to_plane()
    send_right(2)
    left.to_line()
    send_right(3)
    left.finish()
    means = left.out[DATA_LEFT:UNIT_LEFT, :] * (1.0 / rows_all)
    for i in range(BLOCKS):
        mean_ref[0:1, i * NB:(i + 1) * NB] = means[i:i + 1, :]
    for r, c, at in segments(LEFT, DATA_LEFT, UNIT_LEFT):
        c_ref[r:r + 8, c:c + NB] = left.out[at:at + 8, :]
    metric(0, BLOCKS // 2)

    receive(1)
    for r, c, at in segments(RIGHT, UNIT_RIGHT, UNIT_RIGHT):
        right.p[at:at + 8, :] = gram_ref[r:r + 8, c:c + NB]
    right.to_sibling()

    cut_block = BLOCKS // 2
    row = lax.broadcasted_iota(jnp.int32, (NB, NB), 0)
    col = lax.broadcasted_iota(jnp.int32, (NB, NB), 1)

    def step(k, _):
        @pl.when(k == 1)
        def _():
            right.to_plane()
            left.drain()
            rows_of(0, 0, PEERS - 1).wait_send()
            rows_of(1, 0, PEERS - 1).wait_send()
            indices.wait_send()

        @pl.when(k == 3)
        def _():
            right.to_line()

        @pl.when(k == cut_block)
        def _():
            right.finish()
            for r, c, at in segments(RIGHT, UNIT_RIGHT, UNIT_RIGHT):
                c_ref[r:r + 8, c:c + NB] = right.out[at:at + 8, :]
            metric(cut_block, BLOCKS)
            r = lax.broadcasted_iota(jnp.int32, (CUT, CUT), 0)
            c = lax.broadcasted_iota(jnp.int32, (CUT, CUT), 1)
            gram_ref[0:CUT, 0:CUT] = jnp.where(r >= c, c_ref[0:CUT, 0:CUT], 0.0)
            upper = jnp.dot(gram_ref[0:CUT, 0:CUT], c_ref[0:CUT, CUT:], precision=HI, preferred_element_type=F32)
            c_ref[0:CUT, CUT:] = upper
            c_ref[CUT:, 0:CUT] = -lax.dot_general(c_ref[0:CUT, CUT:], gram_ref[0:CUT, 0:CUT], contract_rows,
                                                  precision=HI, preferred_element_type=F32)
            c_ref[CUT:, CUT:] = c_ref[CUT:, CUT:] - lax.dot_general(
                c_ref[0:CUT, CUT:], c_ref[0:CUT, CUT:], contract_rows, precision=HI, preferred_element_type=F32)

        off = pl.multiple_of(k * NB, NB)
        diag = c_ref.at[pl.ds(off, NB), pl.ds(off, NB)]
        rows = factor_block([diag[8 * q:8 * q + 8, :] for q in range(NB // 8)])
        for q in range(NB // 8):
            t_ref[8 * q:8 * q + 8, :] = rows[q]
        t = jnp.where(row >= col, t_ref[...], 0.0)

        @pl.when(k < cut_block)
        def _():
            c_ref[pl.ds(off, NB), 0:CUT] = jnp.dot(
                t, c_ref[pl.ds(off, NB), 0:CUT], precision=HI, preferred_element_type=F32)

        @pl.when(k >= cut_block)
        def _():
            c_ref[pl.ds(off, NB), :] = jnp.dot(
                t, c_ref[pl.ds(off, NB), :], precision=HI, preferred_element_type=F32)

        c_ref[pl.ds(off, NB), pl.ds(off, NB)] = t

        for now in range(BLOCKS - 1):
            if now == cut_block - 1:
                continue

            @pl.when(k == now)
            def _(now=now):
                at, nxt = now * NB, (now + 1) * NB
                end = CUT if now < cut_block else N
                u = c_ref[at:nxt, nxt:end]
                prod = lax.dot_general(u, c_ref[at:nxt, 0:nxt], contract_rows, precision=HI,
                                       preferred_element_type=F32)
                if now:
                    c_ref[nxt:end, 0:at] = c_ref[nxt:end, 0:at] - prod[:, 0:at]
                c_ref[nxt:end, at:nxt] = -prod[:, at:nxt]
                for r in range(nxt, end, 2 * NB):
                    h = min(2 * NB, end - r)
                    prod = lax.dot_general(u[:, r - nxt:r - nxt + h], c_ref[at:nxt, r:end], contract_rows,
                                           precision=HI, preferred_element_type=F32)
                    c_ref[r:r + h, r:end] = c_ref[r:r + h, r:end] - prod
        return 0

    lax.fori_loop(0, BLOCKS, step, 0)
    for i in range(BLOCKS):
        r = lax.broadcasted_iota(jnp.int32, (NB, N), 0) + i * NB
        c = lax.broadcasted_iota(jnp.int32, (NB, N), 1)
        a = i * NB
        out_ref[a:a + NB, :] = jnp.where(r >= c, c_ref[a:a + NB, :], 0.0).astype(jnp.bfloat16)

    right.drain()


def inverse_factor(pair_scale, row_scale, rows_all, anchor, wanted, descriptors):
    dma = pltpu.SemaphoreType.DMA

    def sum_scratch(unit, piece):
        half = PLANE * unit
        return [
            pltpu.VMEM((NC * half, NB), F32),
            pltpu.VMEM((NC * half, NB), F32),
            pltpu.VMEM((half, NB), F32),
            pltpu.VMEM((half, NB), F32),
            pltpu.VMEM((PLANE, unit, NB), F32),
            pltpu.VMEM((NZ * piece, NB), F32),
            pltpu.VMEM((NZ, piece, NB), F32),
            pltpu.VMEM((NZ * piece, NB), F32),
            dma((8, PLANE)),
            dma((4,)),
        ]

    return pl.pallas_call(
        functools.partial(factor_kernel, pair_scale, row_scale, rows_all),
        out_shape=[jax.ShapeDtypeStruct((N, N), jnp.bfloat16), jax.ShapeDtypeStruct((8, N), F32)],
        in_specs=[pl.BlockSpec(memory_space=pltpu.VMEM)] * 3,
        out_specs=[pl.BlockSpec(memory_space=pltpu.VMEM)] * 2,
        scratch_shapes=[
            pltpu.VMEM((2, PEERS, 2 * CAP, CUT // 2), jnp.bfloat16),
            pltpu.VMEM((2, PEERS, 2 * CAP, CUT // 2), jnp.bfloat16),
            pltpu.VMEM((PEERS, 1, NB), F32),
            pltpu.VMEM((PEERS * CAP, NB), F32),
            pltpu.VMEM((PEERS * CAP, N), jnp.bfloat16),
            pltpu.VMEM((PEERS * CAP, N), jnp.bfloat16),
            pltpu.VMEM((N, N), F32),
            pltpu.VMEM((N, N), F32),
            pltpu.VMEM((NB, NB), F32),
            dma((2,)), dma((2, NX)), dma((1,)), dma((1,)),
        ] + sum_scratch(UNIT_LEFT, PIECE_LEFT) + sum_scratch(UNIT_RIGHT, PIECE_RIGHT),
        compiler_params=pltpu.CompilerParams(
            collective_id=1, has_side_effects=True, vmem_limit_bytes=56 << 20
        ),
    )(anchor, wanted, descriptors)


def whiten_kernel(db_ref, mean_ref, inv_ref, out_ref):
    centered = (db_ref[...].astype(F32) - mean_ref[0:1, :]).astype(jnp.bfloat16)
    block = 2 * NB
    parts = []
    energy = 0.0
    for a in range(0, N, block):
        b = a + block
        part = lax.dot_general(centered[:, :b], inv_ref[a:b, :b], (((1,), (1,)), ((), ())), preferred_element_type=F32)
        energy = energy + jnp.sum(part * part, axis=1, keepdims=True)
        parts.append(part)
    scale = lax.rsqrt(energy * (1.0 / N) + norm_epsilon)
    for i, part in enumerate(parts):
        out_ref[:, i * block:(i + 1) * block] = (part * scale).astype(jnp.bfloat16)


def whiten(database, col_mean, inverse):
    rows, width = database.shape
    tile = 256
    return pl.pallas_call(
        whiten_kernel,
        grid=(rows // tile,),
        out_shape=jax.ShapeDtypeStruct((rows, width), jnp.bfloat16),
        in_specs=[
            pl.BlockSpec((tile, width), lambda i: (i, 0)),
            pl.BlockSpec((8, width), lambda i: (0, 0)),
            pl.BlockSpec((width, width), lambda i: (0, 0)),
        ],
        out_specs=pl.BlockSpec((tile, width), lambda i: (i, 0)),
        compiler_params=pltpu.CompilerParams(vmem_limit_bytes=60 << 20),
    )(database, col_mean, inverse)


def shards(descriptors, database, anchor_row, partner_row, block_counts):
    local_rows = descriptors.shape[0]
    peer_count = partner_row.shape[1]
    slot_count = partner_row.shape[2]
    devices = lax.axis_size("dp") * lax.axis_size("mp")
    pairs_all = PAIRS_DEV * devices
    rows_all = local_rows * devices
    slot_iota = lax.broadcasted_iota(jnp.int32, (peer_count, slot_count), 1)
    live_slots = slot_iota < block_counts[0][:, None]
    room = ((0, 0), (0, NB - slot_count))
    wanted = jnp.pad(jnp.where(live_slots, partner_row[0], -1).astype(F32), room)[:, None, :]
    anchor = jnp.pad(jnp.where(live_slots, anchor_row[0], -1).astype(F32), room)[:, None, :]
    inverse, col_mean = inverse_factor(
        1.0 / pairs_all,
        shrink_weight / rows_all,
        rows_all,
        anchor,
        wanted,
        descriptors,
    )
    return whiten(database, col_mean, inverse)


def solution(mesh):
    placed = (
        P(("dp", "mp"), None),
        P(("dp", "mp"), None),
        P(("dp", "mp"), None, None),
        P(("dp", "mp"), None, None),
        P(("dp", "mp"), None),
    )
    return jax.shard_map(
        shards, mesh=mesh, in_specs=placed, out_specs=P(("dp", "mp"), None), check_vma=False
    )
```

```python
import functools

import jax
import jax.numpy as jnp
from jax import lax
from jax.experimental import pallas as pl
from jax.experimental.pallas import tpu as pltpu
from jax.sharding import PartitionSpec as P

PAIRS_DEV = 1024


shrink_weight = 0.5
ridge_term = 0.05
norm_epsilon = 1e-06
contract_rows = (((0,), (0,)), ((), ()))

N = 1024
NB = 128
F32 = jnp.float32
HI = lax.Precision.HIGHEST
MESH = pl.DeviceIdType.MESH

def lane_bcast(x, c):
    return jnp.take_along_axis(x, jnp.full(x.shape, c, jnp.int32), axis=1, mode="promise_in_bounds")


def row_bcast(x, i):
    return jnp.broadcast_to(x[i:i + 1, :], x.shape)


def factor_block(rows):
    lane = lax.broadcasted_iota(jnp.int32, (8, NB), 1)
    sub = lax.broadcasted_iota(jnp.int32, (8, NB), 0)
    count = len(rows)
    for q in range(count):
        base = 8 * q
        inside = (lane >= base) & (lane < base + 8)
        own = [row_bcast(rows[q], i) for i in range(8)]
        d = {}
        for j in range(8):
            for i in range(j, 8):
                d[i, j] = lane_bcast(own[i], base + j)
        w = [jnp.where(inside, jnp.where(lane == base + i, 1.0, 0.0), own[i]) for i in range(8)]
        ahead = q + 1 < count
        v = [lane_bcast(rows[q + 1], base + j) for j in range(8)] if ahead else None
        inv, scale, low = [], [], {}
        for j in range(8):
            s = lax.rsqrt(d[j, j])
            r = s * s
            inv.append(r)
            scale.append(s)
            for i in range(j + 1, 8):
                low[i, j] = d[i, j] * r
            for i in range(j + 1, 8):
                for k in range(j + 1, i + 1):
                    d[i, k] = d[i, k] - low[i, j] * d[k, j]
            for i in range(j + 1, 8):
                w[i] = w[i] - low[i, j] * w[j]
                if ahead:
                    v[i] = v[i] - low[i, j] * v[j]
        if ahead:
            following = jnp.where(inside, 0.0, rows[q + 1])
            for j in range(8):
                following = following - v[j] * (inv[j] * w[j])
        g = [None] * 8
        for i in range(7, -1, -1):
            acc = inv[i] * w[i]
            for j in range(i + 1, 8):
                acc = acc - low[j, i] * g[j]
            g[i] = acc
        out = scale[0] * w[0]
        for i in range(1, 8):
            out = jnp.where(sub == i, scale[i] * w[i], out)
        rows[q] = out
        for t in range(q + 2, count):
            acc = jnp.where(inside, 0.0, rows[t])
            for j in range(8):
                acc = acc - lane_bcast(rows[t], base + j) * g[j]
            rows[t] = acc
        if ahead:
            rows[q + 1] = following
    return rows


NX, NY, NZ, NC = 4, 4, 8, 2
PLANE = NX * NY
BLOCKS = N // NB
CAP = 24
GROUP = NZ * NC
PEERS = NX * GROUP
CUT = N // 2
LEFT = [(i, j) for j in range(BLOCKS // 2) for i in range(j + 1)]
RIGHT = [(i, j) for j in range(BLOCKS // 2, BLOCKS) for i in range(j + 1)]
DATA_LEFT = len(LEFT) * NB // (NC * PLANE)
UNIT_LEFT = DATA_LEFT + 8
UNIT_RIGHT = len(RIGHT) * NB // (NC * PLANE)
PIECE_LEFT, PIECE_RIGHT = 8, 16


def segments(blocks, data, unit):
    found = []
    for b, (i, j) in enumerate(blocks):
        for s in range(0, NB, 8):
            flat = b * NB + s
            found.append((i * NB + s, j * NB, flat // data * unit + flat % data))
    return found


def one_hot_rows(index, count):
    lane = lax.broadcasted_iota(jnp.int32, (count, NB), 1).astype(F32)
    parts = [jnp.where(index == lane + float(NB * c), 1.0, 0.0).astype(jnp.bfloat16) for c in range(N // NB)]
    return jnp.concatenate(parts, axis=1)


def rem(a, b):
    return a % b if isinstance(a, int) else lax.rem(a, b)


def div(a, b):
    return a // b if isinstance(a, int) else lax.div(a, b)


def rows_at(base, count):
    return pl.ds(pl.multiple_of(base, 8), count)


class Sum:
    def __init__(self, unit, piece, p_ref, out_ref, half, r0, r1, zb, r2, gz, near, far):
        self.unit, self.piece, self.half_rows = unit, piece, PLANE * unit
        self.p, self.out, self.half, self.r0, self.r1 = p_ref, out_ref, half, r0, r1
        self.zb, self.r2, self.gz, self.near, self.far = zb, r2, gz, near, far
        dp, self.y = lax.axis_index("dp"), lax.axis_index("mp")
        self.core, self.z, self.x = rem(dp, NC), rem(div(dp, NC), NZ), div(dp, NC * NZ)
        self.sibling = (dp + 1 - 2 * self.core, self.y)
        self.mine = self.x * NY + self.y

    def plane(self, o):
        return rem(self.x + div(o, NY), NX), rem(self.y + rem(o, NY), NY)

    def plane_from(self, o):
        return rem(self.x + NX - div(o, NY), NX), rem(self.y + NY - rem(o, NY), NY)

    def plane_id(self, o):
        tx, ty = self.plane(o)
        return ((tx * NZ + self.z) * NC + self.core, ty)

    def line_id(self, o):
        return ((self.x * NZ + rem(self.z + o, NZ)) * NC + self.core, self.y)

    def near_copy(self, pair, o, src, dst, target):
        return pltpu.make_async_remote_copy(
            src_ref=src, dst_ref=dst, send_sem=self.near.at[2 * pair, 0], recv_sem=self.near.at[2 * pair + 1, o],
            device_id=target, device_id_type=MESH)

    def far_copy(self, pair, src, dst, target):
        return pltpu.make_async_remote_copy(
            src_ref=src, dst_ref=dst, send_sem=self.far.at[2 * pair], recv_sem=self.far.at[2 * pair + 1],
            device_id=target, device_id_type=MESH)

    def unit_at(self, o):
        tx, ty = self.plane(o)
        return (tx * NY + ty) * self.unit

    def copy0(self, o):
        at = self.unit_at(o)
        src = self.p.at[rows_at((1 - self.core) * self.half_rows + at, self.unit)]
        return self.near_copy(0, o, src, self.r0.at[rows_at(at, self.unit)], self.sibling)

    def copy1(self, o):
        return self.near_copy(1, 0, self.half.at[rows_at(self.unit_at(o), self.unit)], self.r1.at[o], self.plane_id(o))

    def copy2(self, o):
        src = self.zb.at[rows_at((rem(self.z + o, NZ)) * self.piece, self.piece)]
        return self.far_copy(0, src, self.r2.at[o], self.line_id(o))

    def copy3(self, o, owner):
        part = self.gz.at[rows_at(owner * self.piece, self.piece)]
        return self.far_copy(1, part, part, self.line_id(o))

    def copy4(self, o, owner):
        dst = self.out.at[rows_at(self.core * self.half_rows + owner * self.unit, self.unit)]
        return self.near_copy(2, o, self.gz.at[pl.ds(0, self.unit)], dst, self.plane_id(o))

    def copy5(self, o, which):
        tx, ty = self.plane_from(o)
        part = self.out.at[rows_at(which * self.half_rows + (tx * NY + ty) * self.unit, self.unit)]
        return self.near_copy(3, 0, part, part, self.sibling)

    def to_sibling(self):
        @pl.loop(0, PLANE)
        def _(i):
            self.copy0((i + 1) % PLANE).start()

        pad = self.zb.shape[0] - self.unit
        self.zb[self.unit:, :] = jnp.zeros((pad, NB), F32)

    def to_plane(self):
        @pl.loop(1, PLANE)
        def _(o):
            self.copy0(o).wait_recv()
            at = self.unit_at(o)
            own = self.p[rows_at(self.core * self.half_rows + at, self.unit), :]
            self.half[rows_at(at, self.unit), :] = own + self.r0[rows_at(at, self.unit), :]
            self.copy1(o).start()

        self.copy0(0).wait_recv()
        at = self.mine * self.unit
        own = self.p[rows_at(self.core * self.half_rows + at, self.unit), :]
        self.zb[0:self.unit, :] = own + self.r0[rows_at(at, self.unit), :]

    def to_line(self):
        got = self.r1.at[pl.ds(1, PLANE - 1)]
        self.near_copy(1, 0, got, got, self.sibling).wait_recv()
        total = self.zb[0:self.unit, :]
        for o in range(1, PLANE):
            total = total + self.r1[o]
        self.zb[0:self.unit, :] = total

        @pl.loop(1, NZ)
        def _(o):
            self.copy2(o).start()

        own = rows_at(self.z * self.piece, self.piece)
        got = self.r2.at[pl.ds(1, NZ - 1)]
        self.far_copy(0, got, got, self.sibling).wait_recv()
        total = self.zb[own, :]
        for o in range(1, NZ):
            total = total + self.r2[o]
        self.gz[own, :] = total

        @pl.loop(1, NZ)
        def _(o):
            self.copy3(o, self.z).start()

        got = self.gz.at[pl.ds(0, (NZ - 1) * self.piece)]
        self.far_copy(1, got, got, self.sibling).wait_recv()

        @pl.loop(1, PLANE)
        def _(o):
            self.copy4(o, self.mine).start()

        self.out[rows_at(self.core * self.half_rows + self.mine * self.unit, self.unit), :] = self.gz[0:self.unit, :]
        self.copy5(0, self.core).start()

    def finish(self):
        @pl.loop(1, PLANE)
        def _(o):
            tx, ty = self.plane_from(o)
            self.copy4(o, tx * NY + ty).wait_recv()
            self.copy5(o, self.core).start()

        got = self.out.at[pl.ds(0, self.half_rows)]
        self.near_copy(3, 0, got, got, self.sibling).wait_recv()

    def drain(self):
        whole = self.p.at[pl.ds(0, self.half_rows)]
        others = self.p.at[pl.ds(0, self.half_rows - self.unit)]
        line = self.zb.at[pl.ds(0, (NZ - 1) * self.piece)]
        self.near_copy(0, 0, whole, whole, self.sibling).wait_send()
        self.near_copy(1, 0, others, others, self.sibling).wait_send()
        self.far_copy(0, line, line, self.sibling).wait_send()
        self.far_copy(1, line, line, self.sibling).wait_send()
        self.near_copy(2, 0, others, others, self.sibling).wait_send()
        self.near_copy(3, 0, whole, whole, self.sibling).wait_send()


def factor_kernel(pair_scale, row_scale, rows_all, anchor_ref, wanted_ref, desc_ref, out_ref, mean_ref,
                  sbuf, rbuf, windex, wcol, part_ref, diff_ref, gram_ref, c_ref, t_ref, s0, q0, s1, q1,
                  *sums):
    dp, y = lax.axis_index("dp"), lax.axis_index("mp")
    core, z, x = rem(dp, NC), rem(div(dp, NC), NZ), div(dp, NC * NZ)
    left = Sum(UNIT_LEFT, PIECE_LEFT, *sums[:10])
    right = Sum(UNIT_RIGHT, PIECE_RIGHT, *sums[10:])

    def peer(ox, o):
        return rem(x + ox, NX) * GROUP + rem(z + div(o, NC), NZ) * NC + rem(core + rem(o, NC), NC)

    def copy_rows(part, ox, target):
        return pltpu.make_async_remote_copy(
            src_ref=sbuf.at[part, target], dst_ref=rbuf.at[part, dp], send_sem=s0.at[part],
            recv_sem=q0.at[part, ox], device_id=(target, y), device_id_type=MESH)

    def rows_of(part, ox, count):
        return pltpu.make_async_remote_copy(
            src_ref=sbuf.at[part, pl.ds(0, count)], dst_ref=rbuf.at[part, pl.ds(0, count)], send_sem=s0.at[part],
            recv_sem=q0.at[part, ox], device_id=left.sibling, device_id_type=MESH)

    def copy_index(target):
        return pltpu.make_async_remote_copy(
            src_ref=wanted_ref.at[target], dst_ref=windex.at[dp], send_sem=s1.at[0], recv_sem=q1.at[0],
            device_id=(target, y), device_id_type=MESH)

    indices = pltpu.make_async_remote_copy(
        src_ref=wanted_ref.at[pl.ds(0, PEERS - 1)], dst_ref=windex.at[pl.ds(0, PEERS - 1)], send_sem=s1.at[0],
        recv_sem=q1.at[0], device_id=left.sibling, device_id_type=MESH)

    barrier = pltpu.get_barrier_semaphore()

    @pl.loop(1, PEERS)
    def _(k):
        pl.semaphore_signal(barrier, inc=1, device_id=(peer(div(k, GROUP), rem(k, GROUP)), y), device_id_type=MESH)

    @pl.loop(1, PLANE)
    def _(o):
        @pl.when(rem(o, NY) != 0)
        def _():
            pl.semaphore_signal(barrier, inc=1, device_id=left.plane_id(o), device_id_type=MESH)

    rows_x = GROUP * CAP

    def gather(ox):
        group = rem(x + ox, NX)
        base = group * rows_x
        for h in range(2):
            count = rows_x // 2
            index = wcol[pl.ds(pl.multiple_of(base + h * count, count), count), :]
            found = jnp.dot(one_hot_rows(index, count), desc_ref[...], preferred_element_type=F32)
            for p in range(GROUP // 2):
                block = found[p * CAP:(p + 1) * CAP, :]
                for part in range(2):
                    a = part * CUT
                    halves = jnp.concatenate([block[:, a:a + CUT // 2], block[:, a + CUT // 2:a + CUT]], axis=0)
                    sbuf[part, group * GROUP + h * (GROUP // 2) + p] = halves.astype(jnp.bfloat16)

    def turn(rows):
        turned = jnp.concatenate([rows.reshape(PEERS, NB), jnp.zeros((NB - PEERS, NB), F32)], axis=0).T
        for p in range(PEERS):
            wcol[p * CAP:(p + 1) * CAP, :] = jnp.broadcast_to(turned[0:CAP, p:p + 1], (CAP, NB))

    turn(anchor_ref[...])
    gather(0)
    pl.semaphore_wait(barrier, PEERS - 1 + PLANE - NX)

    @pl.loop(0, NX)
    def _(ox):
        @pl.loop(0, GROUP)
        def _(o):
            @pl.when(ox * GROUP + o > 0)
            def _():
                copy_rows(0, ox, peer(ox, o)).start()

        @pl.when(ox == 0)
        def _():
            @pl.loop(1, PEERS)
            def _(k):
                copy_index(peer(div(k, GROUP), rem(k, GROUP))).start()

        @pl.when(ox < NX - 1)
        def _():
            gather(ox + 1)

    def send_right(ox):
        @pl.loop(0 if ox else 1, GROUP)
        def _(o):
            copy_rows(1, ox, peer(ox, o)).start()

    tile = 256
    for i in range(0, N, tile):
        gram_ref[i:i + tile, i:] = row_scale * lax.dot_general(
            desc_ref[:, i:i + tile], desc_ref[:, i:], contract_rows, preferred_element_type=F32)
    ones = jnp.ones((8, desc_ref.shape[0]), jnp.bfloat16)
    sums_row = jnp.dot(ones, desc_ref[...], preferred_element_type=F32)
    sub = lax.broadcasted_iota(jnp.int32, (8, NB), 0)
    packed = sums_row[:, 0:NB]
    for i in range(1, BLOCKS):
        packed = jnp.where(sub == i, sums_row[:, i * NB:(i + 1) * NB], packed)
    for u in range(NC * PLANE):
        left.p[u * UNIT_LEFT + DATA_LEFT:(u + 1) * UNIT_LEFT, :] = packed

    windex[dp] = wanted_ref[dp]

    indices.wait_recv()
    turn(windex[...])

    count = 192

    @pl.loop(0, PEERS * CAP // count)
    def _(g):
        at = pl.ds(pl.multiple_of(g * count, count), count)
        found = jnp.dot(one_hot_rows(wcol[at, :], count), desc_ref[...], preferred_element_type=F32)
        part_ref[at, :] = found.astype(jnp.bfloat16)

    rbuf[0, dp] = sbuf[0, dp]
    rbuf[1, dp] = sbuf[1, dp]

    def receive(part):
        a = part * CUT

        @pl.loop(0, NX)
        def _(ox):
            group = rem(x + NX - ox, NX)
            start = ox * rows_x

            @pl.when(ox == 0)
            def _():
                rows_of(part, ox, GROUP - 1).wait_recv()

            @pl.when(ox > 0)
            def _():
                rows_of(part, ox, GROUP).wait_recv()

            if part == 0:
                @pl.when(ox == 2)
                def _():
                    send_right(0)

            @pl.loop(0, GROUP // 2)
            def _(m):
                first = group * GROUP + 2 * m
                blocks = []
                for e in range(2):
                    got = rbuf[part, first + e].astype(F32)
                    blocks.append(jnp.concatenate([got[:CAP], got[CAP:]], axis=1))
                at = pl.multiple_of(first * CAP, 2 * CAP)
                gap = jnp.concatenate(blocks, axis=0) - part_ref[pl.ds(at, 2 * CAP), a:a + CUT].astype(F32)
                to = pl.multiple_of(start + m * 2 * CAP, 2 * CAP)
                diff_ref[pl.ds(to, 2 * CAP), a:a + CUT] = gap.astype(jnp.bfloat16)

            here = pl.ds(pl.multiple_of(start, rows_x), rows_x)
            for i in range(0, a + CUT, tile):
                b = max(i, a)
                gram_ref[i:i + tile, b:a + CUT] = gram_ref[i:i + tile, b:a + CUT] + pair_scale * lax.dot_general(
                    diff_ref[here, i:i + tile], diff_ref[here, b:a + CUT], contract_rows, preferred_element_type=F32)

    def metric(first_block, last_block):
        row = lax.broadcasted_iota(jnp.int32, (NB, NB), 0)
        col = lax.broadcasted_iota(jnp.int32, (NB, NB), 1)
        for i in range(last_block):
            a, b, e = i * NB, max(i, first_block) * NB, last_block * NB
            outer = lax.dot_general(mean_ref[:, a:a + NB], mean_ref[:, b:e], contract_rows,
                                    precision=HI, preferred_element_type=F32)
            c_ref[a:a + NB, b:e] = c_ref[a:a + NB, b:e] - shrink_weight * outer
            if i >= first_block:
                c_ref[a:a + NB, a:a + NB] = c_ref[a:a + NB, a:a + NB] + jnp.where(row == col, ridge_term, 0.0)

    receive(0)
    for r, c, at in segments(LEFT, DATA_LEFT, UNIT_LEFT):
        left.p[at:at + 8, :] = gram_ref[r:r + 8, c:c + NB]
    left.to_sibling()
    c_ref[...] = jnp.zeros((N, N), F32)
    mean_ref[...] = jnp.zeros((8, N), F32)
    left.to_plane()
    send_right(1)
    send_right(2)
    send_right(3)
    left.to_line()
    left.finish()
    means = left.out[DATA_LEFT:UNIT_LEFT, :] * (1.0 / rows_all)
    for i in range(BLOCKS):
        mean_ref[0:1, i * NB:(i + 1) * NB] = means[i:i + 1, :]
    for r, c, at in segments(LEFT, DATA_LEFT, UNIT_LEFT):
        c_ref[r:r + 8, c:c + NB] = left.out[at:at + 8, :]
    metric(0, BLOCKS // 2)

    receive(1)
    for r, c, at in segments(RIGHT, UNIT_RIGHT, UNIT_RIGHT):
        right.p[at:at + 8, :] = gram_ref[r:r + 8, c:c + NB]
    right.to_sibling()

    cut_block = BLOCKS // 2
    row = lax.broadcasted_iota(jnp.int32, (NB, NB), 0)
    col = lax.broadcasted_iota(jnp.int32, (NB, NB), 1)

    def step(k, _):
        @pl.when(k == 0)
        def _():
            right.to_plane()
            left.drain()
            rows_of(0, 0, PEERS - 1).wait_send()
            rows_of(1, 0, PEERS - 1).wait_send()
            indices.wait_send()

        @pl.when(k == 2)
        def _():
            right.to_line()

        @pl.when(k == cut_block)
        def _():
            right.finish()
            for r, c, at in segments(RIGHT, UNIT_RIGHT, UNIT_RIGHT):
                c_ref[r:r + 8, c:c + NB] = right.out[at:at + 8, :]
            metric(cut_block, BLOCKS)
            r = lax.broadcasted_iota(jnp.int32, (CUT, CUT), 0)
            c = lax.broadcasted_iota(jnp.int32, (CUT, CUT), 1)
            gram_ref[0:CUT, 0:CUT] = jnp.where(r >= c, c_ref[0:CUT, 0:CUT], 0.0)
            upper = jnp.dot(gram_ref[0:CUT, 0:CUT], c_ref[0:CUT, CUT:], precision=HI, preferred_element_type=F32)
            c_ref[0:CUT, CUT:] = upper
            c_ref[CUT:, 0:CUT] = -lax.dot_general(c_ref[0:CUT, CUT:], gram_ref[0:CUT, 0:CUT], contract_rows,
                                                  precision=HI, preferred_element_type=F32)
            c_ref[CUT:, CUT:] = c_ref[CUT:, CUT:] - lax.dot_general(
                c_ref[0:CUT, CUT:], c_ref[0:CUT, CUT:], contract_rows, precision=HI, preferred_element_type=F32)

        off = pl.multiple_of(k * NB, NB)
        diag = c_ref.at[pl.ds(off, NB), pl.ds(off, NB)]
        rows = factor_block([diag[8 * q:8 * q + 8, :] for q in range(NB // 8)])
        for q in range(NB // 8):
            t_ref[8 * q:8 * q + 8, :] = rows[q]
        t = jnp.where(row >= col, t_ref[...], 0.0)

        @pl.when(k < cut_block)
        def _():
            c_ref[pl.ds(off, NB), 0:CUT] = jnp.dot(
                t, c_ref[pl.ds(off, NB), 0:CUT], precision=HI, preferred_element_type=F32)

        @pl.when(k >= cut_block)
        def _():
            c_ref[pl.ds(off, NB), :] = jnp.dot(
                t, c_ref[pl.ds(off, NB), :], precision=HI, preferred_element_type=F32)

        c_ref[pl.ds(off, NB), pl.ds(off, NB)] = t

        for now in range(BLOCKS - 1):
            if now == cut_block - 1:
                continue

            @pl.when(k == now)
            def _(now=now):
                at, nxt = now * NB, (now + 1) * NB
                end = CUT if now < cut_block else N
                u = c_ref[at:nxt, nxt:end]
                prod = lax.dot_general(u, c_ref[at:nxt, 0:nxt], contract_rows, precision=HI,
                                       preferred_element_type=F32)
                if now:
                    c_ref[nxt:end, 0:at] = c_ref[nxt:end, 0:at] - prod[:, 0:at]
                c_ref[nxt:end, at:nxt] = -prod[:, at:nxt]
                for r in range(nxt, end, 2 * NB):
                    h = min(2 * NB, end - r)
                    prod = lax.dot_general(u[:, r - nxt:r - nxt + h], c_ref[at:nxt, r:end], contract_rows,
                                           precision=HI, preferred_element_type=F32)
                    c_ref[r:r + h, r:end] = c_ref[r:r + h, r:end] - prod
        return 0

    lax.fori_loop(0, BLOCKS, step, 0)
    for i in range(BLOCKS):
        r = lax.broadcasted_iota(jnp.int32, (NB, N), 0) + i * NB
        c = lax.broadcasted_iota(jnp.int32, (NB, N), 1)
        a = i * NB
        out_ref[a:a + NB, :] = jnp.where(r >= c, c_ref[a:a + NB, :], 0.0).astype(jnp.bfloat16)

    right.drain()


def inverse_factor(pair_scale, row_scale, rows_all, anchor, wanted, descriptors):
    dma = pltpu.SemaphoreType.DMA

    def sum_scratch(unit, piece):
        half = PLANE * unit
        return [
            pltpu.VMEM((NC * half, NB), F32),
            pltpu.VMEM((NC * half, NB), F32),
            pltpu.VMEM((half, NB), F32),
            pltpu.VMEM((half, NB), F32),
            pltpu.VMEM((PLANE, unit, NB), F32),
            pltpu.VMEM((NZ * piece, NB), F32),
            pltpu.VMEM((NZ, piece, NB), F32),
            pltpu.VMEM((NZ * piece, NB), F32),
            dma((8, PLANE)),
            dma((4,)),
        ]

    return pl.pallas_call(
        functools.partial(factor_kernel, pair_scale, row_scale, rows_all),
        out_shape=[jax.ShapeDtypeStruct((N, N), jnp.bfloat16), jax.ShapeDtypeStruct((8, N), F32)],
        in_specs=[pl.BlockSpec(memory_space=pltpu.VMEM)] * 3,
        out_specs=[pl.BlockSpec(memory_space=pltpu.VMEM)] * 2,
        scratch_shapes=[
            pltpu.VMEM((2, PEERS, 2 * CAP, CUT // 2), jnp.bfloat16),
            pltpu.VMEM((2, PEERS, 2 * CAP, CUT // 2), jnp.bfloat16),
            pltpu.VMEM((PEERS, 1, NB), F32),
            pltpu.VMEM((PEERS * CAP, NB), F32),
            pltpu.VMEM((PEERS * CAP, N), jnp.bfloat16),
            pltpu.VMEM((PEERS * CAP, N), jnp.bfloat16),
            pltpu.VMEM((N, N), F32),
            pltpu.VMEM((N, N), F32),
            pltpu.VMEM((NB, NB), F32),
            dma((2,)), dma((2, NX)), dma((1,)), dma((1,)),
        ] + sum_scratch(UNIT_LEFT, PIECE_LEFT) + sum_scratch(UNIT_RIGHT, PIECE_RIGHT),
        compiler_params=pltpu.CompilerParams(
            collective_id=1, has_side_effects=True, vmem_limit_bytes=56 << 20
        ),
    )(anchor, wanted, descriptors)


def whiten_kernel(db_ref, mean_ref, inv_ref, out_ref):
    centered = (db_ref[...].astype(F32) - mean_ref[0:1, :]).astype(jnp.bfloat16)
    block = 2 * NB
    parts = []
    energy = 0.0
    for a in range(0, N, block):
        b = a + block
        part = lax.dot_general(centered[:, :b], inv_ref[a:b, :b], (((1,), (1,)), ((), ())), preferred_element_type=F32)
        energy = energy + jnp.sum(part * part, axis=1, keepdims=True)
        parts.append(part)
    scale = lax.rsqrt(energy * (1.0 / N) + norm_epsilon)
    for i, part in enumerate(parts):
        out_ref[:, i * block:(i + 1) * block] = (part * scale).astype(jnp.bfloat16)


def whiten(database, col_mean, inverse):
    rows, width = database.shape
    tile = 256
    return pl.pallas_call(
        whiten_kernel,
        grid=(rows // tile,),
        out_shape=jax.ShapeDtypeStruct((rows, width), jnp.bfloat16),
        in_specs=[
            pl.BlockSpec((tile, width), lambda i: (i, 0)),
            pl.BlockSpec((8, width), lambda i: (0, 0)),
            pl.BlockSpec((width, width), lambda i: (0, 0)),
        ],
        out_specs=pl.BlockSpec((tile, width), lambda i: (i, 0)),
        compiler_params=pltpu.CompilerParams(vmem_limit_bytes=60 << 20),
    )(database, col_mean, inverse)


def shards(descriptors, database, anchor_row, partner_row, block_counts):
    local_rows = descriptors.shape[0]
    peer_count = partner_row.shape[1]
    slot_count = partner_row.shape[2]
    devices = lax.axis_size("dp") * lax.axis_size("mp")
    pairs_all = PAIRS_DEV * devices
    rows_all = local_rows * devices
    slot_iota = lax.broadcasted_iota(jnp.int32, (peer_count, slot_count), 1)
    live_slots = slot_iota < block_counts[0][:, None]
    room = ((0, 0), (0, NB - slot_count))
    wanted = jnp.pad(jnp.where(live_slots, partner_row[0], -1).astype(F32), room)[:, None, :]
    anchor = jnp.pad(jnp.where(live_slots, anchor_row[0], -1).astype(F32), room)[:, None, :]
    inverse, col_mean = inverse_factor(
        1.0 / pairs_all,
        shrink_weight / rows_all,
        rows_all,
        anchor,
        wanted,
        descriptors,
    )
    return whiten(database, col_mean, inverse)


def solution(mesh):
    placed = (
        P(("dp", "mp"), None),
        P(("dp", "mp"), None),
        P(("dp", "mp"), None, None),
        P(("dp", "mp"), None, None),
        P(("dp", "mp"), None),
    )
    return jax.shard_map(
        shards, mesh=mesh, in_specs=placed, out_specs=P(("dp", "mp"), None), check_vma=False
    )
```
